128 devices in a mesh: group: 4 (over x_lo, core), blk: 32 (over z, y, x_hi).
Axes of the slice: x: 4 (x_hi: 2, x_lo: 2; x = x_hi * 2 + x_lo), y: 4, z: 4, core: 2. Of those that a mesh axis runs over, the one named last changes fastest.
Arguments:
- image_emb: bfloat16 [49152, 1280], P(('group', 'blk')), may hold values from -6 to 6
- text_emb: bfloat16 [49152, 1280], P(('group', 'blk')), may hold values from -1 to 1
- positive: int32 [49152], P(('group', 'blk')), may hold values from 0 to 383, as said below
- logit_scale: float32 [1], replicated, may hold values from 10 to 20
Outputs:
- loss: float32 [1], replicated
- image_grad: float32 [49152, 1280], P(('group', 'blk'))
- text_grad: float32 [49152, 1280], P(('group', 'blk'))
The draws below stay inside these ranges and needn't reach their ends.
Inputs may be any that keep to these rules, and one draw needn't show every extreme that they name: `positive`: within every aligned block of 384 rows the values are a permutation of 0 to 383.
All inputs are finite; a program needn't handle non-finite values.
Results may differ from the reference program's by a relative error of at most 0.0022.
Values may be sent and summed in bfloat16 or wider, within the bound.
A program may use at most 128 MiB of HBM per device.

```python
import math
import jax
import jax.numpy as jnp
from jax import lax

D = 1280
ROWS = 384
WIN = 8
GROUPS = 4
LOOP = 32
BATCH = 49152


def paired_base(key):
    perm_keys = jax.random.split(jax.random.fold_in(key, 101), BATCH // ROWS)
    orders = jax.vmap(lambda one_key: jax.random.permutation(one_key, ROWS))(perm_keys)
    shared = jnp.clip(jax.random.normal(jax.random.fold_in(key, 102), (BATCH, D), jnp.float32), -5.0, 5.0)
    return (orders.astype(jnp.int32), shared)


def draw_positive(key, part):
    orders, shared = paired_base(key)
    return orders.reshape(BATCH).astype(jnp.int32)


def draw_image_emb(key, part):
    orders, shared = paired_base(key)
    key = jax.random.fold_in(key, 2)
    noise = jnp.clip(jax.random.normal(key, (BATCH, D), jnp.float32), -5.0, 5.0)
    values = (0.7 * shared + 0.7 * noise) * D ** (-0.5)
    return jnp.clip(values, -6.0, 6.0).astype(jnp.bfloat16)


def draw_text_emb(key, part):
    orders, shared = paired_base(key)
    key = jax.random.fold_in(key, 3)
    noise = jnp.clip(jax.random.normal(key, (BATCH, D), jnp.float32), -5.0, 5.0)
    values = (0.7 * shared + 0.7 * noise) * D ** (-0.5)
    target = jnp.arange(BATCH, dtype=jnp.int32) // ROWS * ROWS + orders.reshape(BATCH)
    placed = jnp.zeros((BATCH, D), jnp.float32).at[target].set(values)
    return jnp.clip(placed, -1.0, 1.0).astype(jnp.bfloat16)


def setup_inputs(seed: int = 0) -> dict:
    keys = jax.random.split(jax.random.key(seed), 5)
    return {
        "image_emb": draw_image_emb(jax.random.fold_in(keys[4], 71), 0),
        "text_emb": draw_text_emb(jax.random.fold_in(keys[4], 71), 0),
        "positive": draw_positive(jax.random.fold_in(keys[4], 71), 0),
        "logit_scale": jnp.clip(jnp.exp(jax.random.uniform(keys[3], (1,), jnp.float32, math.log(10.0), math.log(20.0))), 10.0, 20.0),
    }


def block_scores(left_rows, right_rows, factor):
    return factor * jnp.dot(left_rows, right_rows.T, preferred_element_type=jnp.float32)


def window_text(device, offset):
    if offset == 0:
        return device
    group_id = device // LOOP
    loop_id = device % LOOP
    return ((group_id - 1) % GROUPS) * LOOP + (loop_id - offset + 1) % LOOP


def window_image(device, offset):
    if offset == 0:
        return device
    group_id = device // LOOP
    loop_id = device % LOOP
    return ((group_id + 1) % GROUPS) * LOOP + (loop_id + offset - 1) % LOOP


def reference(image_emb, text_emb, positive, logit_scale):
    factor = logit_scale[0]
    block_count = GROUPS * LOOP
    image_blocks = image_emb.reshape(block_count, ROWS, D)
    text_blocks = text_emb.reshape(block_count, ROWS, D)
    pair_index = positive.reshape(block_count, ROWS)
    columns = jnp.arange(ROWS, dtype=jnp.int32)
    devices = jnp.arange(block_count, dtype=jnp.int32)

    def pair_mask(index_row):
        return (columns[None, :] == index_row[:, None]).astype(jnp.float32)

    def row_side(device):
        score_blocks = [block_scores(image_blocks[device], text_blocks[window_text(device, offset)], factor) for offset in range(WIN)]
        joined = jnp.concatenate(score_blocks, axis=1)
        row_peak = jnp.max(joined, axis=1, keepdims=True)
        row_log = row_peak[:, 0] + jnp.log(jnp.sum(jnp.exp(joined - row_peak), axis=1))
        chosen = jnp.sum(score_blocks[0] * pair_mask(pair_index[device]))
        return row_log, chosen

    def column_side(device):
        score_blocks = [block_scores(image_blocks[window_image(device, offset)], text_blocks[device], factor) for offset in range(WIN)]
        joined = jnp.concatenate(score_blocks, axis=0)
        col_peak = jnp.max(joined, axis=0, keepdims=True)
        return col_peak[0, :] + jnp.log(jnp.sum(jnp.exp(joined - col_peak), axis=0))

    row_lse, chosen = lax.map(row_side, devices)
    col_lse = lax.map(column_side, devices)
    loss_value = (jnp.sum(row_lse) + jnp.sum(col_lse) - 2.0 * jnp.sum(chosen)) / (2.0 * BATCH)
    loss = jnp.reshape(loss_value, (1,))

    def image_side(device):
        running = jnp.zeros((ROWS, D), jnp.float32)
        for offset in range(WIN):
            source = window_text(device, offset)
            scores = block_scores(image_blocks[device], text_blocks[source], factor)
            weight = jnp.exp(scores - row_lse[device][:, None]) + jnp.exp(scores - col_lse[source][None, :])
            if offset == 0:
                weight = weight - 2.0 * pair_mask(pair_index[device])
            running = running + jnp.dot(weight.astype(jnp.bfloat16), text_blocks[source], preferred_element_type=jnp.float32)
        return factor * running

    def text_side(device):
        running = jnp.zeros((ROWS, D), jnp.float32)
        for offset in range(WIN):
            source = window_image(device, offset)
            scores = block_scores(image_blocks[source], text_blocks[device], factor)
            weight = jnp.exp(scores - row_lse[source][:, None]) + jnp.exp(scores - col_lse[device][None, :])
            if offset == 0:
                weight = weight - 2.0 * pair_mask(pair_index[device])
            running = running + jnp.dot(weight.astype(jnp.bfloat16).T, image_blocks[source], preferred_element_type=jnp.float32)
        return factor * running

    image_grad = lax.map(image_side, devices).reshape(BATCH, D)
    text_grad = lax.map(text_side, devices).reshape(BATCH, D)
    return (loss, image_grad, text_grad)
```

```python
import functools

import jax
import jax.numpy as jnp
from jax import lax
from jax.experimental import pallas as pl
from jax.experimental.pallas import tpu as pltpu
from jax.sharding import PartitionSpec as P

MESH = pl.DeviceIdType.MESH
F32 = jnp.float32
BF16 = jnp.bfloat16
R = 384
D = 1280
H = D // 2
NC = 4
CH = R // NC
ST = 48
LOW = -1e30
RING = 16


def rcopy(src, dst, ss, rs, dev):
    return pltpu.make_async_remote_copy(
        src_ref=src, dst_ref=dst, send_sem=ss, recv_sem=rs, device_id=dev, device_id_type=MESH
    )


def dot_t(a, b):
    return lax.dot_general(a, b, (((1,), (1,)), ((), ())), preferred_element_type=F32)


def dot_n(a, b):
    return lax.dot_general(a, b, (((1,), (0,)), ((), ())), preferred_element_type=F32)


def merge(parts):
    peak = functools.reduce(jnp.maximum, [m for m, _ in parts])
    total = sum(s * jnp.exp(m - peak) for m, s in parts)
    return peak, total


def tile_of(peak, total):
    row = lax.broadcasted_iota(jnp.int32, (8, peak.shape[1]), 0)
    return jnp.where(row == 0, peak, total)


def pair_of(tile):
    return tile[0:1, :], tile[1:2, :]


def kernel(
    scale_ref, image_ref, text_ref, pos_ref,
    terms_ref, image_out, text_out,
    texts, images, scores, own_scores, weights, weights_t, own_weights_t,
    packed, col_column, row_part, row_diag, col_part, col_diag,
    row_peer, row_owner, row_back, col_peer,
    part1, part2, part3, stash1, stash3, part_in, half_in,
    grad_send, grad_in, image_acc, text_acc,
    local_sem, fetch_ss, fetch_rs, fwd_ss, relay_ss, img_ss, img_rs,
    row_ss, row_rs, col_ss, col_rs,
    half_ss, half_rs, part_ss, part_rs, back_ss, grad_ss, grad_rs,
):
    group = lax.axis_index("group")
    blk = lax.axis_index("blk")
    xh = blk % 2
    big_y = blk // 2
    y = big_y % 4
    factor = scale_ref[0]

    def at_row(step):
        return (group, ((big_y + step + RING) % RING) * 2 + xh)

    up, down = at_row(1), at_row(-1)
    behind = (group + 3) % 4
    ahead = (group + 1) % 4
    same, other = blk, big_y * 2 + (1 - xh)
    handler_same, handler_other = (behind, same), (behind, other)
    owner_same, owner_other = (ahead, same), (ahead, other)
    peer = (group, other)

    text_copy = pltpu.make_async_copy(text_ref, texts.at[0], local_sem.at[0])
    image_copy = pltpu.make_async_copy(image_ref, images.at[pl.ds(2 * R, R)], local_sem.at[1])
    text_copy.start()
    image_copy.start()

    barrier = pltpu.get_barrier_semaphore()
    partners = [at_row(s) for s in (1, 2, 3, 4, -1, -2, -3, -4)]
    partners += [handler_same, handler_other, owner_same, owner_other, peer]
    for dev in partners:
        pl.semaphore_signal(barrier, inc=1, device_id=dev, device_id_type=MESH)
    pl.semaphore_wait(barrier, len(partners))

    def part_of(ref, slot, half, c):
        return ref.at[slot, pl.ds(c * CH, CH), pl.ds(half * H, H)]

    wrap_up = y // 3
    up_slot = 1 + 3 * wrap_up
    up_far = at_row(1 + 3 * wrap_up)
    far = at_row(3)

    def own_copy(stream, slot, half, c, dev):
        return rcopy(
            part_of(texts, 0, half, c), part_of(texts, slot, half, c),
            fetch_ss.at[stream, c], fetch_rs.at[slot, half, c], dev,
        )

    def arrived(slot, half, c):
        ref = part_of(texts, slot, half, c)
        rcopy(ref, ref, fetch_ss.at[0, c], fetch_rs.at[slot, half, c], up).wait_recv()

    def fwd_copy(stream, slot, half, c, dev):
        return rcopy(
            part_of(texts, slot, half, c), part_of(texts, 2, half, c),
            fwd_ss.at[stream, c], fetch_rs.at[2, half, c], dev,
        )

    def relay_copy(half, c):
        return rcopy(
            part_of(texts, 4, half, c), part_of(texts, 1, half, c),
            relay_ss.at[half, c], fetch_rs.at[1, half, c], at_row(-3),
        )

    text_copy.wait()
    for c in range(NC):
        own_copy(0, up_slot, 0, c, up_far).start()
        own_copy(1, 3, 1, c, far).start()
    image_copy.wait()
    own_image = images.at[pl.ds(2 * R, R)]
    to_other = rcopy(own_image, images.at[pl.ds(R, R)], img_ss.at[1], img_rs.at[1], handler_other)
    to_same = rcopy(own_image, images.at[pl.ds(0, R)], img_ss.at[0], img_rs.at[0], handler_same)
    to_other.start()
    to_same.start()
    for c in range(NC):
        own_copy(2, up_slot, 1, c, up_far).start()
        own_copy(3, 3, 0, c, far).start()

    def pack_columns(ref, width, rows):
        x = ref[rows, :]
        peak = jnp.max(x, axis=1, keepdims=True)
        total = jnp.sum(jnp.exp(x - peak), axis=1, keepdims=True)
        lane = lax.broadcasted_iota(jnp.int32, (ST, 128), 1)
        packed[rows, :] = jnp.where(lane == 0, peak, total)
        return jnp.max(x, axis=0, keepdims=True)

    def block_stats(ref, width):
        def first(i, peak):
            rows = pl.ds(pl.multiple_of(i * ST, ST), ST)
            return jnp.maximum(peak, pack_columns(ref, width, rows))

        peak = lax.fori_loop(0, R // ST, first, jnp.full((1, width), LOW, F32))

        def second(i, total):
            rows = pl.ds(pl.multiple_of(i * ST, ST), ST)
            return total + jnp.sum(jnp.exp(ref[rows, :] - peak), axis=0, keepdims=True)

        total = lax.fori_loop(0, R // ST, second, jnp.zeros((1, width), F32))
        col_tile = jnp.transpose(packed[...])[0:8, :]
        return (peak, total), col_tile

    own_scores[...] = factor * dot_t(texts[0], images[pl.ds(2 * R, R), :])
    (diag_peak, diag_total), diag_cols = block_stats(own_scores, R)
    row_diag[...] = tile_of(diag_peak, diag_total)
    col_diag[...] = diag_cols

    def forward(c, _):
        @pl.when(y == 3)
        def _():
            arrived(4, 0, c)
            relay_copy(0, c).start()

        arrived(1, 0, c)
        fwd_copy(0, 1, 0, c, up).start()
        arrived(3, 1, c)
        fwd_copy(1, 3, 1, c, down).start()
        return 0

    lax.fori_loop(0, NC, forward, 0)

    @pl.when(y == 3)
    def _():
        def relay(c, _):
            arrived(4, 1, c)
            relay_copy(1, c).start()
            return 0

        lax.fori_loop(0, NC, relay, 0)

    to_other.wait_recv()
    to_same.wait_recv()

    def block_scores(d, row_state):
        def column(n, _):
            cols = pl.ds(pl.multiple_of(n * 256, 256), 256)
            scores[d, :, cols] = factor * dot_t(texts[d], images[cols, :])
            return 0

        lax.fori_loop(0, 3, column, 0)
        if d in (0, 3):
            @pl.when(xh == (1 if d == 0 else 0))
            def _():
                scores[d, :, pl.ds(R, R)] = jnp.full((R, R), LOW, F32)

        stats, cols = block_stats(scores.at[d], 2 * R)
        if d == 0:
            col_part[0] = tile_of(*merge([pair_of(cols), pair_of(col_diag[...])]))
        else:
            col_part[d] = cols
        return stats if row_state is None else merge([row_state, stats])

    state = block_scores(0, None)
    for c in range(NC):
        arrived(1, 1, c)
    state = block_scores(1, state)
    for c in range(NC):
        arrived(3, 0, c)
    state = block_scores(3, state)
    for half in range(2):
        for c in range(NC):
            arrived(2, half, c)
    state = block_scores(2, state)

    both = tile_of(*state)
    row_part[0] = both[:, 0:R]
    row_part[1] = both[:, R:2 * R]
    sends = []
    steps = (1, 2, 3, -1, -2, -3)
    for k, step in enumerate(steps):
        low, high = max(0, -step), min(4, 4 - step)
        sends.append(rcopy(
            col_part.at[pl.ds(low, high - low)],
            col_peer.at[k, pl.ds(low + step, high - low)],
            col_ss.at[k], col_rs.at[k], at_row(step),
        ))
    sends.append(rcopy(row_part, row_peer, row_ss.at[0], row_rs.at[0], peer))
    sends.append(rcopy(row_part.at[0], row_back.at[0], row_ss.at[1], row_rs.at[1], owner_same))
    sends.append(rcopy(row_part.at[1], row_back.at[1], row_ss.at[2], row_rs.at[2], owner_other))
    sends.append(rcopy(row_diag, row_owner.at[0], row_ss.at[3], row_rs.at[3], handler_same))
    sends.append(rcopy(row_diag, row_owner.at[1], row_ss.at[4], row_rs.at[4], handler_other))
    for copy in sends:
        copy.start()
    for copy in sends:
        copy.wait_recv()

    def lse(parts):
        peak, total = merge(parts)
        return peak + jnp.log(total)

    row_lse = jnp.concatenate(
        [lse([pair_of(row_part[k]), pair_of(row_peer[1 - k]), pair_of(row_owner[k])]) for k in range(2)],
        axis=1,
    )
    own_row_lse = lse([pair_of(row_diag[...]), pair_of(row_back[0]), pair_of(row_back[1])])

    def col_lse(d):
        parts = [pair_of(col_part[d])]
        for k, step in enumerate(steps):
            if 0 <= d - step <= 3:
                parts.append(pair_of(col_peer[k, d]))
        value = lse(parts)
        col_column[d] = jnp.transpose(jnp.broadcast_to(value, (128, R)))
        return value

    def block_weights(d):
        def step(i, _):
            rows = pl.ds(pl.multiple_of(i * ST, ST), ST)
            x = scores[d, rows, :]
            col = jnp.concatenate([col_column[d, rows, :]] * (2 * R // 128), axis=1)
            weights[d, rows, pl.ds(0, 2 * R)] = (jnp.exp(x - row_lse) + jnp.exp(x - col)).astype(BF16)
            return 0

        lax.fori_loop(0, R // ST, step, 0)

    def text_part(d, half):
        return dot_n(weights[d, :, pl.ds(0, 2 * R)], images[pl.ds(0, 2 * R), pl.ds(half * H, H)])

    def flip(d):
        def step(i, _):
            rows = pl.ds(pl.multiple_of(i * 128, 128), 128)
            weights_t[rows, pl.ds(d * R, R)] = jnp.transpose(weights[d, :, rows])
            return 0

        lax.fori_loop(0, 6, step, 0)

    wrap_down = 1 - (y + 3) // 4
    down_slot = 2 * wrap_down
    down_far = at_row(-1 - 3 * wrap_down)
    back_far = at_row(-3)

    def cut(ref, half, c):
        return ref.at[pl.ds(c * CH, CH), pl.ds(half * H, H)]

    def half_copy(half, c, dev):
        return rcopy(
            cut(part2, half, c), half_in.at[half, pl.ds(c * CH, CH)],
            half_ss.at[half, c], half_rs.at[half, c], dev,
        )

    def part_copy(ref, stream, slot, half, c, dev):
        return rcopy(
            cut(ref, half, c), part_of(part_in, slot, half, c),
            part_ss.at[stream, half, c], part_rs.at[slot, half, c], dev,
        )

    def part_arrived(slot, half, c):
        ref = part_of(part_in, slot, half, c)
        rcopy(ref, ref, part_ss.at[0, half, c], part_rs.at[slot, half, c], up).wait_recv()

    def back_copy(half, c):
        return rcopy(
            part_of(part_in, 2, half, c), part_of(part_in, 0, half, c),
            back_ss.at[half, c], part_rs.at[0, half, c], at_row(3),
        )

    col_lse(2)
    block_weights(2)
    part2[:, pl.ds(0, H)] = text_part(2, 0).astype(BF16)
    for c in range(NC):
        half_copy(0, c, down).start()
    part2[:, pl.ds(H, H)] = text_part(2, 1).astype(BF16)
    for c in range(NC):
        half_copy(1, c, up).start()
    col_lse(1)
    block_weights(1)
    part1[:, pl.ds(H, H)] = text_part(1, 1).astype(BF16)
    for c in range(NC):
        part_copy(part1, 0, down_slot, 1, c, down_far).start()
    col_lse(3)
    block_weights(3)
    part3[:, pl.ds(0, H)] = text_part(3, 0).astype(BF16)
    for c in range(NC):
        part_copy(part3, 1, 1, 0, c, back_far).start()
    stash1[...] = text_part(1, 0)
    stash3[...] = text_part(3, 1)
    own_col_lse = col_lse(0)
    block_weights(0)
    for d in range(4):
        flip(d)

    def image_part(k):
        def column(n, _):
            cols = pl.ds(pl.multiple_of(n * 256, 256), 256)
            total = dot_n(weights_t[pl.ds(k * R, R), pl.ds(0, R)], texts[0, :, cols])
            for d in range(1, 4):
                total += dot_n(weights_t[pl.ds(k * R, R), pl.ds(d * R, R)], texts[d, :, cols])
            grad_send[k, :, cols] = total.astype(BF16)
            return 0

        lax.fori_loop(0, 5, column, 0)

    grad_other = rcopy(grad_send.at[1], grad_in.at[1], grad_ss.at[1], grad_rs.at[1], owner_other)
    grad_same = rcopy(grad_send.at[0], grad_in.at[0], grad_ss.at[0], grad_rs.at[0], owner_same)
    image_part(1)
    grad_other.start()
    image_part(0)
    grad_same.start()

    @pl.when(y == 0)
    def _():
        def relay(c, _):
            part_arrived(2, 1, c)
            back_copy(1, c).start()
            return 0

        lax.fori_loop(0, NC, relay, 0)

    def add_halves(c, _):
        rows = pl.ds(pl.multiple_of(c * CH, CH), CH)
        half_copy(0, c, down).wait_recv()
        part1[rows, pl.ds(0, H)] = (stash1[rows, :] + half_in[0, rows, :].astype(F32)).astype(BF16)
        part_copy(part1, 0, down_slot, 0, c, down_far).start()
        half_copy(1, c, up).wait_recv()
        part3[rows, pl.ds(H, H)] = (stash3[rows, :] + half_in[1, rows, :].astype(F32)).astype(BF16)
        part_copy(part3, 1, 1, 1, c, back_far).start()
        return 0

    lax.fori_loop(0, NC, add_halves, 0)

    @pl.when(y == 0)
    def _():
        def relay(c, _):
            part_arrived(2, 0, c)
            back_copy(0, c).start()
            return 0

        lax.fori_loop(0, NC, relay, 0)

    positive = pos_ref[...]
    column = lax.broadcasted_iota(jnp.int32, (R, R), 0)
    mask = column == positive
    x = own_scores[...]
    chosen = jnp.sum(jnp.where(mask, x, 0.0))
    own_col = jnp.concatenate([col_column[0]] * (R // 128), axis=1)
    own_w = jnp.exp(x - own_row_lse) + jnp.exp(x - own_col)
    weights[0, :, pl.ds(2 * R, R)] = jnp.where(mask, own_w - 2.0, own_w).astype(BF16)
    for i in range(3):
        own_weights_t[pl.ds(i * 128, 128), :] = jnp.transpose(weights[0, :, pl.ds(2 * R + i * 128, 128)])
    terms = jnp.sum(own_row_lse) + jnp.sum(own_col_lse) - 2.0 * chosen
    terms_ref[...] = jnp.full((8, 128), terms, F32)

    def own_column(n, _):
        cols = pl.ds(pl.multiple_of(n * 256, 256), 256)
        text_acc[:, cols] = dot_n(weights[0], images[:, cols])
        image_acc[:, cols] = dot_n(own_weights_t[...], texts[0, :, cols])
        return 0

    lax.fori_loop(0, 5, own_column, 0)

    grad_other.wait_recv()
    grad_same.wait_recv()

    def out_copy(acc, out, k, c):
        rows = pl.ds(pl.multiple_of(c * CH, CH), CH)
        return pltpu.make_async_copy(acc.at[rows], out.at[rows], local_sem.at[2 + k * NC + c])

    def finish_image(c, _):
        rows = pl.ds(pl.multiple_of(c * CH, CH), CH)
        image_acc[rows, :] += grad_in[0, rows, :].astype(F32) + grad_in[1, rows, :].astype(F32)
        out_copy(image_acc, image_out, 0, c).start()
        return 0

    lax.fori_loop(0, NC, finish_image, 0)

    def finish_text(c, _):
        rows = pl.ds(pl.multiple_of(c * CH, CH), CH)
        for slot in range(2):
            for half in range(2):
                part_arrived(slot, half, c)
        text_acc[rows, :] += part_in[0, rows, :].astype(F32) + part_in[1, rows, :].astype(F32)
        out_copy(text_acc, text_out, 1, c).start()
        return 0

    lax.fori_loop(0, NC, finish_text, 0)

    to_other.wait_send()
    to_same.wait_send()
    for copy in sends:
        copy.wait_send()
    grad_other.wait_send()
    grad_same.wait_send()

    def drain(c, _):
        own_copy(0, up_slot, 0, c, up_far).wait_send()
        own_copy(1, 3, 1, c, far).wait_send()
        own_copy(2, up_slot, 1, c, up_far).wait_send()
        own_copy(3, 3, 0, c, far).wait_send()
        fwd_copy(0, 1, 0, c, up).wait_send()
        fwd_copy(1, 3, 1, c, down).wait_send()
        half_copy(0, c, down).wait_send()
        half_copy(1, c, up).wait_send()
        for half in range(2):
            part_copy(part1, 0, down_slot, half, c, down_far).wait_send()
            part_copy(part3, 1, 1, half, c, back_far).wait_send()

        @pl.when(y == 3)
        def _():
            relay_copy(0, c).wait_send()
            relay_copy(1, c).wait_send()

        @pl.when(y == 0)
        def _():
            back_copy(0, c).wait_send()
            back_copy(1, c).wait_send()

        out_copy(image_acc, image_out, 0, c).wait()
        out_copy(text_acc, text_out, 1, c).wait()
        return 0

    lax.fori_loop(0, NC, drain, 0)


def on_device(image_emb, text_emb, positive, logit_scale):
    vmem, dma = pltpu.VMEM, pltpu.SemaphoreType.DMA
    terms, image_total, text_total = pl.pallas_call(
        kernel,
        out_shape=(
            jax.ShapeDtypeStruct((8, 128), F32),
            jax.ShapeDtypeStruct((R, D), F32),
            jax.ShapeDtypeStruct((R, D), F32),
        ),
        in_specs=[
            pl.BlockSpec(memory_space=pltpu.SMEM),
            pl.BlockSpec(memory_space=pl.ANY),
            pl.BlockSpec(memory_space=pl.ANY),
            pl.BlockSpec(memory_space=pltpu.VMEM),
        ],
        out_specs=(
            pl.BlockSpec(memory_space=pltpu.VMEM),
            pl.BlockSpec(memory_space=pl.ANY),
            pl.BlockSpec(memory_space=pl.ANY),
        ),
        scratch_shapes=[
            vmem((5, R, D), BF16),
            vmem((3 * R, D), BF16),
            vmem((4, R, 2 * R), F32),
            vmem((R, R), F32),
            vmem((4, R, 3 * R), BF16),
            vmem((2 * R, 4 * R), BF16),
            vmem((R, R), BF16),
            vmem((R, 128), F32),
            vmem((4, R, 128), F32),
            vmem((2, 8, R), F32),
            vmem((8, R), F32),
            vmem((4, 8, R), F32),
            vmem((8, R), F32),
            vmem((2, 8, R), F32),
            vmem((2, 8, R), F32),
            vmem((2, 8, R), F32),
            vmem((6, 4, 8, R), F32),
            vmem((R, D), BF16),
            vmem((R, D), BF16),
            vmem((R, D), BF16),
            vmem((R, H), F32),
            vmem((R, H), F32),
            vmem((3, R, D), BF16),
            vmem((2, R, H), BF16),
            vmem((2, R, D), BF16),
            vmem((2, R, D), BF16),
            vmem((R, D), F32),
            vmem((R, D), F32),
            dma((2 + 2 * NC,)),
            dma((4, NC)),
            dma((5, 2, NC)),
            dma((2, NC)),
            dma((2, NC)),
            dma((2,)),
            dma((2,)),
            dma((5,)),
            dma((5,)),
            dma((6,)),
            dma((6,)),
            dma((2, NC)),
            dma((2, NC)),
            dma((2, 2, NC)),
            dma((3, 2, NC)),
            dma((2, NC)),
            dma((2,)),
            dma((2,)),
        ],
        compiler_params=pltpu.CompilerParams(
            collective_id=0, has_side_effects=True, vmem_limit_bytes=56 * 1024 * 1024
        ),
    )(logit_scale, image_emb, text_emb, positive.reshape(1, R))
    batch_size = R * lax.axis_size("group") * lax.axis_size("blk")
    loss = lax.psum(terms[0, 0:1], ("group", "blk")) / (2.0 * batch_size)
    factor = logit_scale[0]
    return (loss, factor * image_total, factor * text_total)


def solution(mesh):
    placed = (P(("group", "blk"), None), P(("group", "blk"), None), P(("group", "blk")), P())
    return jax.shard_map(
        on_device,
        mesh=mesh,
        in_specs=placed,
        out_specs=(P(), P(("group", "blk"), None), P(("group", "blk"), None)),
        check_vma=False,
    )
```

```python
import functools

import jax
import jax.numpy as jnp
from jax import lax
from jax.experimental import pallas as pl
from jax.experimental.pallas import tpu as pltpu
from jax.sharding import PartitionSpec as P

MESH = pl.DeviceIdType.MESH
F32 = jnp.float32
BF16 = jnp.bfloat16
R = 384
D = 1280
H = D // 2
NC = 4
CH = R // NC
ST = 48
LOW = -1e30
RING = 16


def rcopy(src, dst, ss, rs, dev):
    return pltpu.make_async_remote_copy(
        src_ref=src, dst_ref=dst, send_sem=ss, recv_sem=rs, device_id=dev, device_id_type=MESH
    )


def dot_t(a, b):
    return lax.dot_general(a, b, (((1,), (1,)), ((), ())), preferred_element_type=F32)


def dot_n(a, b):
    return lax.dot_general(a, b, (((1,), (0,)), ((), ())), preferred_element_type=F32)


def merge(parts):
    peak = functools.reduce(jnp.maximum, [m for m, _ in parts])
    total = sum(s * jnp.exp(m - peak) for m, s in parts)
    return peak, total


def tile_of(peak, total):
    row = lax.broadcasted_iota(jnp.int32, (8, peak.shape[1]), 0)
    return jnp.where(row == 0, peak, total)


def pair_of(tile):
    return tile[0:1, :], tile[1:2, :]


def kernel(
    scale_ref, image_ref, text_ref, pos_ref,
    loss_ref, image_out, text_out,
    texts, images, scores, own_scores, weights, weights_t, own_weights_t,
    packed, col_column, row_part, row_diag, col_part, col_diag,
    row_peer, row_owner, row_back, col_peer,
    part1, part2, part3, stash1, stash3, part_in, half_in,
    grad_send, grad_in, image_acc, text_acc,
    local_sem, fetch_ss, fetch_rs, fwd_ss, relay_ss, img_ss, img_rs,
    row_ss, row_rs, col_ss, col_rs,
    half_ss, half_rs, part_ss, part_rs, back_ss, grad_ss, grad_rs,
    loss_out, loss_in, loss_ss, loss_rs,
):
    group = lax.axis_index("group")
    blk = lax.axis_index("blk")
    xh = blk % 2
    big_y = blk // 2
    y = big_y % 4
    factor = scale_ref[0]

    def at_row(step):
        return (group, ((big_y + step + RING) % RING) * 2 + xh)

    up, down = at_row(1), at_row(-1)
    behind = (group + 3) % 4
    ahead = (group + 1) % 4
    same, other = blk, big_y * 2 + (1 - xh)
    handler_same, handler_other = (behind, same), (behind, other)
    owner_same, owner_other = (ahead, same), (ahead, other)
    peer = (group, other)

    text_copy = pltpu.make_async_copy(text_ref, texts.at[0], local_sem.at[0])
    image_copy = pltpu.make_async_copy(image_ref, images.at[pl.ds(2 * R, R)], local_sem.at[1])
    text_copy.start()
    image_copy.start()

    barrier = pltpu.get_barrier_semaphore()
    partners = [at_row(s) for s in (1, 2, 3, 4, -1, -2, -3, -4)]
    partners += [handler_same, handler_other, owner_same, owner_other, peer]
    opposite = ((group + 2) % 4, same)
    partners += [at_row(8), opposite]
    for dev in partners:
        pl.semaphore_signal(barrier, inc=1, device_id=dev, device_id_type=MESH)
    pl.semaphore_wait(barrier, len(partners))

    def part_of(ref, slot, half, c):
        return ref.at[slot, pl.ds(c * CH, CH), pl.ds(half * H, H)]

    wrap_up = y // 3
    up_slot = 1 + 3 * wrap_up
    up_far = at_row(1 + 3 * wrap_up)
    far = at_row(3)

    def own_copy(stream, slot, half, c, dev):
        return rcopy(
            part_of(texts, 0, half, c), part_of(texts, slot, half, c),
            fetch_ss.at[stream, c], fetch_rs.at[slot, half, c], dev,
        )

    def arrived(slot, half, c):
        ref = part_of(texts, slot, half, c)
        rcopy(ref, ref, fetch_ss.at[0, c], fetch_rs.at[slot, half, c], up).wait_recv()

    def fwd_copy(stream, slot, half, c, dev):
        return rcopy(
            part_of(texts, slot, half, c), part_of(texts, 2, half, c),
            fwd_ss.at[stream, c], fetch_rs.at[2, half, c], dev,
        )

    def relay_copy(half, c):
        return rcopy(
            part_of(texts, 4, half, c), part_of(texts, 1, half, c),
            relay_ss.at[half, c], fetch_rs.at[1, half, c], at_row(-3),
        )

    text_copy.wait()
    for c in range(NC):
        own_copy(0, up_slot, 0, c, up_far).start()
        own_copy(1, 3, 1, c, far).start()
    image_copy.wait()
    own_image = images.at[pl.ds(2 * R, R)]
    to_other = rcopy(own_image, images.at[pl.ds(R, R)], img_ss.at[1], img_rs.at[1], handler_other)
    to_same = rcopy(own_image, images.at[pl.ds(0, R)], img_ss.at[0], img_rs.at[0], handler_same)
    to_other.start()
    to_same.start()
    for c in range(NC):
        own_copy(2, up_slot, 1, c, up_far).start()
        own_copy(3, 3, 0, c, far).start()

    def pack_columns(ref, width, rows):
        x = ref[rows, :]
        peak = jnp.max(x, axis=1, keepdims=True)
        total = jnp.sum(jnp.exp(x - peak), axis=1, keepdims=True)
        lane = lax.broadcasted_iota(jnp.int32, (ST, 128), 1)
        packed[rows, :] = jnp.where(lane == 0, peak, total)
        return jnp.max(x, axis=0, keepdims=True)

    def block_stats(ref, width):
        def first(i, peak):
            rows = pl.ds(pl.multiple_of(i * ST, ST), ST)
            return jnp.maximum(peak, pack_columns(ref, width, rows))

        peak = lax.fori_loop(0, R // ST, first, jnp.full((1, width), LOW, F32))

        def second(i, total):
            rows = pl.ds(pl.multiple_of(i * ST, ST), ST)
            return total + jnp.sum(jnp.exp(ref[rows, :] - peak), axis=0, keepdims=True)

        total = lax.fori_loop(0, R // ST, second, jnp.zeros((1, width), F32))
        col_tile = jnp.transpose(packed[...])[0:8, :]
        return (peak, total), col_tile

    own_scores[...] = factor * dot_t(texts[0], images[pl.ds(2 * R, R), :])
    positive = pos_ref[...].reshape(1, R)
    mask = lax.broadcasted_iota(jnp.int32, (R, R), 0) == positive
    chosen = jnp.sum(jnp.where(mask, own_scores[...], 0.0))
    (diag_peak, diag_total), diag_cols = block_stats(own_scores, R)
    row_diag[...] = tile_of(diag_peak, diag_total)
    col_diag[...] = diag_cols

    def forward(c, _):
        @pl.when(y == 3)
        def _():
            arrived(4, 0, c)
            relay_copy(0, c).start()

        arrived(1, 0, c)
        fwd_copy(0, 1, 0, c, up).start()
        arrived(3, 1, c)
        fwd_copy(1, 3, 1, c, down).start()
        return 0

    lax.fori_loop(0, NC, forward, 0)

    @pl.when(y == 3)
    def _():
        def relay(c, _):
            arrived(4, 1, c)
            relay_copy(1, c).start()
            return 0

        lax.fori_loop(0, NC, relay, 0)

    to_other.wait_recv()
    to_same.wait_recv()

    def block_scores(d, row_state):
        def column(n, _):
            cols = pl.ds(pl.multiple_of(n * 256, 256), 256)
            scores[d, :, cols] = factor * dot_t(texts[d], images[cols, :])
            return 0

        lax.fori_loop(0, 3, column, 0)
        if d in (0, 3):
            @pl.when(xh == (1 if d == 0 else 0))
            def _():
                scores[d, :, pl.ds(R, R)] = jnp.full((R, R), LOW, F32)

        stats, cols = block_stats(scores.at[d], 2 * R)
        if d == 0:
            col_part[0] = tile_of(*merge([pair_of(cols), pair_of(col_diag[...])]))
        else:
            col_part[d] = cols
        return stats if row_state is None else merge([row_state, stats])

    state = block_scores(0, None)
    for c in range(NC):
        arrived(1, 1, c)
    state = block_scores(1, state)
    for c in range(NC):
        arrived(3, 0, c)
    state = block_scores(3, state)
    for half in range(2):
        for c in range(NC):
            arrived(2, half, c)
    state = block_scores(2, state)

    both = tile_of(*state)
    row_part[0] = both[:, 0:R]
    row_part[1] = both[:, R:2 * R]
    sends = []
    steps = (1, 2, 3, -1, -2, -3)
    for k, step in enumerate(steps):
        low, high = max(0, -step), min(4, 4 - step)
        sends.append(rcopy(
            col_part.at[pl.ds(low, high - low)],
            col_peer.at[k, pl.ds(low + step, high - low)],
            col_ss.at[k], col_rs.at[k], at_row(step),
        ))
    sends.append(rcopy(row_part, row_peer, row_ss.at[0], row_rs.at[0], peer))
    sends.append(rcopy(row_part.at[0], row_back.at[0], row_ss.at[1], row_rs.at[1], owner_same))
    sends.append(rcopy(row_part.at[1], row_back.at[1], row_ss.at[2], row_rs.at[2], owner_other))
    sends.append(rcopy(row_diag, row_owner.at[0], row_ss.at[3], row_rs.at[3], handler_same))
    sends.append(rcopy(row_diag, row_owner.at[1], row_ss.at[4], row_rs.at[4], handler_other))
    for copy in sends:
        copy.start()
    for copy in sends:
        copy.wait_recv()

    mates = [peer, (group + 1 - 2 * (group % 2), same), opposite]
    for bit in (1, 2, 4, 8):
        mates.append(at_row(bit - 2 * bit * ((big_y // bit) % 2)))

    def loss_copy(k):
        return rcopy(loss_out.at[k], loss_in.at[k], loss_ss.at[k], loss_rs.at[k], mates[k])

    def loss_round(k, value=None):
        if k > 0:
            loss_copy(k - 1).wait_recv()
            value = loss_out[k - 1] + loss_in[k - 1]
        loss_out[k] = value
        if k < len(mates):
            loss_copy(k).start()

    def lse(parts):
        peak, total = merge(parts)
        return peak + jnp.log(total)

    row_lse = jnp.concatenate(
        [lse([pair_of(row_part[k]), pair_of(row_peer[1 - k]), pair_of(row_owner[k])]) for k in range(2)],
        axis=1,
    )
    own_row_lse = lse([pair_of(row_diag[...]), pair_of(row_back[0]), pair_of(row_back[1])])

    def col_lse(d):
        parts = [pair_of(col_part[d])]
        for k, step in enumerate(steps):
            if 0 <= d - step <= 3:
                parts.append(pair_of(col_peer[k, d]))
        value = lse(parts)
        col_column[d] = jnp.transpose(jnp.broadcast_to(value, (128, R)))
        return value

    def block_weights(d):
        def step(i, _):
            rows = pl.ds(pl.multiple_of(i * ST, ST), ST)
            x = scores[d, rows, :]
            col = jnp.concatenate([col_column[d, rows, :]] * (2 * R // 128), axis=1)
            weights[d, rows, pl.ds(0, 2 * R)] = (jnp.exp(x - row_lse) + jnp.exp(x - col)).astype(BF16)
            return 0

        lax.fori_loop(0, R // ST, step, 0)

    def text_part(d, half):
        return dot_n(weights[d, :, pl.ds(0, 2 * R)], images[pl.ds(0, 2 * R), pl.ds(half * H, H)])

    def flip(d):
        def step(i, _):
            rows = pl.ds(pl.multiple_of(i * 128, 128), 128)
            weights_t[rows, pl.ds(d * R, R)] = jnp.transpose(weights[d, :, rows])
            return 0

        lax.fori_loop(0, 6, step, 0)

    wrap_down = 1 - (y + 3) // 4
    down_slot = 2 * wrap_down
    down_far = at_row(-1 - 3 * wrap_down)
    back_far = at_row(-3)

    def cut(ref, half, c):
        return ref.at[pl.ds(c * CH, CH), pl.ds(half * H, H)]

    def half_copy(half, c, dev):
        return rcopy(
            cut(part2, half, c), half_in.at[half, pl.ds(c * CH, CH)],
            half_ss.at[half, c], half_rs.at[half, c], dev,
        )

    def part_copy(ref, stream, slot, half, c, dev):
        return rcopy(
            cut(ref, half, c), part_of(part_in, slot, half, c),
            part_ss.at[stream, half, c], part_rs.at[slot, half, c], dev,
        )

    def part_arrived(slot, half, c):
        ref = part_of(part_in, slot, half, c)
        rcopy(ref, ref, part_ss.at[0, half, c], part_rs.at[slot, half, c], up).wait_recv()

    def back_copy(half, c):
        return rcopy(
            part_of(part_in, 2, half, c), part_of(part_in, 0, half, c),
            back_ss.at[half, c], part_rs.at[0, half, c], at_row(3),
        )

    col_lse(2)
    block_weights(2)
    part2[:, pl.ds(0, H)] = text_part(2, 0).astype(BF16)
    for c in range(NC):
        half_copy(0, c, down).start()
    part2[:, pl.ds(H, H)] = text_part(2, 1).astype(BF16)
    for c in range(NC):
        half_copy(1, c, up).start()
    own_col_lse = col_lse(0)
    terms = jnp.sum(own_row_lse) + jnp.sum(own_col_lse) - 2.0 * chosen
    loss_round(0, jnp.full((8, 128), terms, F32))
    col_lse(1)
    block_weights(1)
    part1[:, pl.ds(H, H)] = text_part(1, 1).astype(BF16)
    for c in range(NC):
        part_copy(part1, 0, down_slot, 1, c, down_far).start()
    loss_round(1)
    col_lse(3)
    block_weights(3)
    part3[:, pl.ds(0, H)] = text_part(3, 0).astype(BF16)
    for c in range(NC):
        part_copy(part3, 1, 1, 0, c, back_far).start()
    stash1[...] = text_part(1, 0)
    stash3[...] = text_part(3, 1)
    loss_round(2)
    block_weights(0)
    for d in range(4):
        flip(d)

    def image_part(k):
        def column(n, _):
            cols = pl.ds(pl.multiple_of(n * 256, 256), 256)
            total = dot_n(weights_t[pl.ds(k * R, R), pl.ds(0, R)], texts[0, :, cols])
            for d in range(1, 4):
                total += dot_n(weights_t[pl.ds(k * R, R), pl.ds(d * R, R)], texts[d, :, cols])
            grad_send[k, :, cols] = total.astype(BF16)
            return 0

        lax.fori_loop(0, 5, column, 0)

    grad_other = rcopy(grad_send.at[1], grad_in.at[1], grad_ss.at[1], grad_rs.at[1], owner_other)
    grad_same = rcopy(grad_send.at[0], grad_in.at[0], grad_ss.at[0], grad_rs.at[0], owner_same)
    image_part(1)
    grad_other.start()
    loss_round(3)
    image_part(0)
    grad_same.start()
    loss_round(4)

    @pl.when(y == 0)
    def _():
        def relay(c, _):
            part_arrived(2, 1, c)
            back_copy(1, c).start()
            return 0

        lax.fori_loop(0, NC, relay, 0)

    def add_halves(c, _):
        rows = pl.ds(pl.multiple_of(c * CH, CH), CH)
        half_copy(0, c, down).wait_recv()
        part1[rows, pl.ds(0, H)] = (stash1[rows, :] + half_in[0, rows, :].astype(F32)).astype(BF16)
        part_copy(part1, 0, down_slot, 0, c, down_far).start()
        half_copy(1, c, up).wait_recv()
        part3[rows, pl.ds(H, H)] = (stash3[rows, :] + half_in[1, rows, :].astype(F32)).astype(BF16)
        part_copy(part3, 1, 1, 1, c, back_far).start()
        return 0

    lax.fori_loop(0, NC, add_halves, 0)
    loss_round(5)

    @pl.when(y == 0)
    def _():
        def relay(c, _):
            part_arrived(2, 0, c)
            back_copy(0, c).start()
            return 0

        lax.fori_loop(0, NC, relay, 0)

    x = own_scores[...]
    own_col = jnp.concatenate([col_column[0]] * (R // 128), axis=1)
    own_w = jnp.exp(x - own_row_lse) + jnp.exp(x - own_col)
    weights[0, :, pl.ds(2 * R, R)] = jnp.where(mask, own_w - 2.0, own_w).astype(BF16)
    for i in range(3):
        own_weights_t[pl.ds(i * 128, 128), :] = jnp.transpose(weights[0, :, pl.ds(2 * R + i * 128, 128)])
    loss_round(6)

    def own_column(n, _):
        cols = pl.ds(pl.multiple_of(n * 256, 256), 256)
        text_acc[:, cols] = dot_n(weights[0], images[:, cols])
        image_acc[:, cols] = dot_n(own_weights_t[...], texts[0, :, cols])
        return 0

    lax.fori_loop(0, 5, own_column, 0)

    loss_round(7)
    loss_ref[0] = loss_out[7, 0, 0] * (0.5 / (R * 128))

    grad_other.wait_recv()
    grad_same.wait_recv()

    def out_copy(acc, out, k, c):
        rows = pl.ds(pl.multiple_of(c * CH, CH), CH)
        return pltpu.make_async_copy(acc.at[rows], out.at[rows], local_sem.at[2 + k * NC + c])

    def finish_image(c, _):
        rows = pl.ds(pl.multiple_of(c * CH, CH), CH)
        image_acc[rows, :] = factor * (
            image_acc[rows, :] + grad_in[0, rows, :].astype(F32) + grad_in[1, rows, :].astype(F32)
        )
        out_copy(image_acc, image_out, 0, c).start()
        return 0

    lax.fori_loop(0, NC, finish_image, 0)

    def finish_text(c, _):
        rows = pl.ds(pl.multiple_of(c * CH, CH), CH)
        for slot in range(2):
            for half in range(2):
                part_arrived(slot, half, c)
        text_acc[rows, :] = factor * (
            text_acc[rows, :] + part_in[0, rows, :].astype(F32) + part_in[1, rows, :].astype(F32)
        )
        out_copy(text_acc, text_out, 1, c).start()
        return 0

    lax.fori_loop(0, NC, finish_text, 0)

    to_other.wait_send()
    to_same.wait_send()
    for copy in sends:
        copy.wait_send()
    grad_other.wait_send()
    grad_same.wait_send()
    for k in range(len(mates)):
        loss_copy(k).wait_send()

    def drain(c, _):
        own_copy(0, up_slot, 0, c, up_far).wait_send()
        own_copy(1, 3, 1, c, far).wait_send()
        own_copy(2, up_slot, 1, c, up_far).wait_send()
        own_copy(3, 3, 0, c, far).wait_send()
        fwd_copy(0, 1, 0, c, up).wait_send()
        fwd_copy(1, 3, 1, c, down).wait_send()
        half_copy(0, c, down).wait_send()
        half_copy(1, c, up).wait_send()
        for half in range(2):
            part_copy(part1, 0, down_slot, half, c, down_far).wait_send()
            part_copy(part3, 1, 1, half, c, back_far).wait_send()

        @pl.when(y == 3)
        def _():
            relay_copy(0, c).wait_send()
            relay_copy(1, c).wait_send()

        @pl.when(y == 0)
        def _():
            back_copy(0, c).wait_send()
            back_copy(1, c).wait_send()

        out_copy(image_acc, image_out, 0, c).wait()
        out_copy(text_acc, text_out, 1, c).wait()
        return 0

    lax.fori_loop(0, NC, drain, 0)


def on_device(image_emb, text_emb, positive, logit_scale):
    vmem, dma = pltpu.VMEM, pltpu.SemaphoreType.DMA
    return pl.pallas_call(
        kernel,
        out_shape=(
            jax.ShapeDtypeStruct((1,), F32),
            jax.ShapeDtypeStruct((R, D), F32),
            jax.ShapeDtypeStruct((R, D), F32),
        ),
        in_specs=[
            pl.BlockSpec(memory_space=pltpu.SMEM),
            pl.BlockSpec(memory_space=pl.ANY),
            pl.BlockSpec(memory_space=pl.ANY),
            pl.BlockSpec(memory_space=pltpu.VMEM),
        ],
        out_specs=(
            pl.BlockSpec(memory_space=pltpu.SMEM),
            pl.BlockSpec(memory_space=pl.ANY),
            pl.BlockSpec(memory_space=pl.ANY),
        ),
        scratch_shapes=[
            vmem((5, R, D), BF16),
            vmem((3 * R, D), BF16),
            vmem((4, R, 2 * R), F32),
            vmem((R, R), F32),
            vmem((4, R, 3 * R), BF16),
            vmem((2 * R, 4 * R), BF16),
            vmem((R, R), BF16),
            vmem((R, 128), F32),
            vmem((4, R, 128), F32),
            vmem((2, 8, R), F32),
            vmem((8, R), F32),
            vmem((4, 8, R), F32),
            vmem((8, R), F32),
            vmem((2, 8, R), F32),
            vmem((2, 8, R), F32),
            vmem((2, 8, R), F32),
            vmem((6, 4, 8, R), F32),
            vmem((R, D), BF16),
            vmem((R, D), BF16),
            vmem((R, D), BF16),
            vmem((R, H), F32),
            vmem((R, H), F32),
            vmem((3, R, D), BF16),
            vmem((2, R, H), BF16),
            vmem((2, R, D), BF16),
            vmem((2, R, D), BF16),
            vmem((R, D), F32),
            vmem((R, D), F32),
            dma((2 + 2 * NC,)),
            dma((4, NC)),
            dma((5, 2, NC)),
            dma((2, NC)),
            dma((2, NC)),
            dma((2,)),
            dma((2,)),
            dma((5,)),
            dma((5,)),
            dma((6,)),
            dma((6,)),
            dma((2, NC)),
            dma((2, NC)),
            dma((2, 2, NC)),
            dma((3, 2, NC)),
            dma((2, NC)),
            dma((2,)),
            dma((2,)),
            vmem((8, 8, 128), F32),
            vmem((7, 8, 128), F32),
            dma((7,)),
            dma((7,)),
        ],
        compiler_params=pltpu.CompilerParams(
            collective_id=0, has_side_effects=True, vmem_limit_bytes=42 * 1024 * 1024
        ),
    )(logit_scale, image_emb, text_emb, positive)


def solution(mesh):
    placed = (P(("group", "blk"), None), P(("group", "blk"), None), P(("group", "blk")), P())
    return jax.shard_map(
        on_device,
        mesh=mesh,
        in_specs=placed,
        out_specs=(P(), P(("group", "blk"), None), P(("group", "blk"), None)),
        check_vma=False,
    )
```

```python
import functools

import jax
import jax.numpy as jnp
from jax import lax
from jax.experimental import pallas as pl
from jax.experimental.pallas import tpu as pltpu
from jax.sharding import PartitionSpec as P

MESH = pl.DeviceIdType.MESH
F32 = jnp.float32
BF16 = jnp.bfloat16
R = 384
D = 1280
H = D // 2
NC = 3
CH = R // NC
LOW = -1e30
RING = 16


def rcopy(src, dst, ss, rs, dev):
    return pltpu.make_async_remote_copy(
        src_ref=src, dst_ref=dst, send_sem=ss, recv_sem=rs, device_id=dev, device_id_type=MESH
    )


def dot_t(a, b):
    return lax.dot_general(a, b, (((1,), (1,)), ((), ())), preferred_element_type=F32)


def dot_n(a, b):
    return lax.dot_general(a, b, (((1,), (0,)), ((), ())), preferred_element_type=F32)


def merge(parts):
    peak = functools.reduce(jnp.maximum, [m for m, _ in parts])
    total = sum(s * jnp.exp(m - peak) for m, s in parts)
    return peak, total


def tile_of(peak, total):
    row = lax.broadcasted_iota(jnp.int32, (8, peak.shape[1]), 0)
    return jnp.where(row == 0, peak, total)


def pair_of(tile):
    return tile[0:1, :], tile[1:2, :]


def kernel(
    scale_ref, image_ref, text_ref, pos_ref,
    loss_ref, image_out, text_out,
    texts, images, scores, own_scores, weights, weights_t, own_weights_t,
    col_column, row_part, row_diag, col_part, col_diag,
    row_peer, row_owner, row_back, col_peer,
    part1, part2, part3, stash1, stash3, part_in, half_in,
    grad_send, grad_in, image_acc, text_acc,
    local_sem, fetch_ss, fetch_rs, fwd_ss, relay_ss, img_ss, img_rs,
    row_ss, row_rs, col_ss, col_rs,
    half_ss, half_rs, part_ss, part_rs, back_ss, grad_ss, grad_rs,
    loss_out, loss_in, loss_ss, loss_rs, pos_vmem,
):
    group = lax.axis_index("group")
    blk = lax.axis_index("blk")
    xh = blk % 2
    big_y = blk // 2
    y = big_y % 4
    factor = scale_ref[0]

    def at_row(step):
        return (group, ((big_y + step + RING) % RING) * 2 + xh)

    up, down = at_row(1), at_row(-1)
    behind = (group + 3) % 4
    ahead = (group + 1) % 4
    same, other = blk, big_y * 2 + (1 - xh)
    handler_same, handler_other = (behind, same), (behind, other)
    owner_same, owner_other = (ahead, same), (ahead, other)
    peer = (group, other)

    text_copy = pltpu.make_async_copy(text_ref, texts.at[0], local_sem.at[0])
    image_copy = pltpu.make_async_copy(image_ref, images.at[pl.ds(2 * R, R)], local_sem.at[1])
    pos_copy = pltpu.make_async_copy(pos_ref, pos_vmem, local_sem.at[2 + 2 * NC])
    text_copy.start()
    pos_copy.start()
    image_copy.start()

    barrier = pltpu.get_barrier_semaphore()
    partners = [at_row(s) for s in (1, 2, 3, 4, -1, -2, -3, -4)]
    partners += [handler_same, handler_other, owner_same, owner_other, peer]
    opposite = ((group + 2) % 4, same)
    partners += [at_row(8), opposite]
    for step in (4, 8, 12):
        partners.append((group, ((big_y + step) % RING) * 2 + (1 - xh)))
    for dev in partners:
        pl.semaphore_signal(barrier, inc=1, device_id=dev, device_id_type=MESH)
    pl.semaphore_wait(barrier, len(partners))

    def part_of(ref, slot, half, c):
        return ref.at[slot, pl.ds(c * CH, CH), pl.ds(half * H, H)]

    wrap_up = y // 3
    up_slot = 1 + 3 * wrap_up
    up_far = at_row(1 + 3 * wrap_up)
    far = at_row(3)

    def own_copy(stream, slot, half, c, dev):
        return rcopy(
            part_of(texts, 0, half, c), part_of(texts, slot, half, c),
            fetch_ss.at[stream, c], fetch_rs.at[slot, half, c], dev,
        )

    def arrived(slot, half, c):
        ref = part_of(texts, slot, half, c)
        rcopy(ref, ref, fetch_ss.at[0, c], fetch_rs.at[slot, half, c], up).wait_recv()

    def fwd_copy(stream, slot, half, c, dev):
        return rcopy(
            part_of(texts, slot, half, c), part_of(texts, 2, half, c),
            fwd_ss.at[stream, c], fetch_rs.at[2, half, c], dev,
        )

    def relay_copy(half, c):
        return rcopy(
            part_of(texts, 4, half, c), part_of(texts, 1, half, c),
            relay_ss.at[half, c], fetch_rs.at[1, half, c], at_row(-3),
        )

    text_copy.wait()
    for c in range(NC):
        own_copy(0, up_slot, 0, c, up_far).start()
        own_copy(1, 3, 1, c, far).start()
    image_copy.wait()
    own_image = images.at[pl.ds(2 * R, R)]
    to_other = rcopy(own_image, images.at[pl.ds(R, R)], img_ss.at[1], img_rs.at[1], handler_other)
    to_same = rcopy(own_image, images.at[pl.ds(0, R)], img_ss.at[0], img_rs.at[0], handler_same)
    to_other.start()
    to_same.start()

    def chunk_stats(ref, cols_ref, start, size):
        rows = pl.ds(start, size)
        lane = lax.broadcasted_iota(jnp.int32, (size, 128), 1)
        x = ref[rows, :]
        peak = jnp.max(x, axis=1, keepdims=True)
        total = jnp.sum(jnp.exp(x - peak), axis=1, keepdims=True)
        cols_ref[:, rows] = jnp.transpose(jnp.where(lane == 0, peak, total))[0:8, :]
        row_peak = jnp.max(x, axis=0, keepdims=True)
        return row_peak, jnp.sum(jnp.exp(x - row_peak), axis=0, keepdims=True)

    own_scores[...] = factor * dot_t(texts[0], images[pl.ds(2 * R, R), :])
    pos_copy.wait()
    positive = pos_vmem[...].reshape(1, R)
    mask = lax.broadcasted_iota(jnp.int32, (R, R), 0) == positive
    chosen = jnp.sum(jnp.where(mask, own_scores[...], 0.0))
    row_diag[...] = tile_of(*chunk_stats(own_scores, col_diag, 0, R))

    def forward(c, _):
        @pl.when(y == 3)
        def _():
            arrived(4, 0, c)
            relay_copy(0, c).start()

        arrived(1, 0, c)
        fwd_copy(0, 1, 0, c, up).start()
        arrived(3, 1, c)
        fwd_copy(1, 3, 1, c, down).start()
        own_copy(2, up_slot, 1, c, up_far).start()
        own_copy(3, 3, 0, c, far).start()
        return 0

    lax.fori_loop(0, NC, forward, 0)

    @pl.when(y == 3)
    def _():
        def relay(c, _):
            arrived(4, 1, c)
            relay_copy(1, c).start()
            return 0

        lax.fori_loop(0, NC, relay, 0)

    to_other.wait_recv()
    to_same.wait_recv()

    def keep_scores(d, start, x):
        rows = pl.ds(start, x.shape[0])
        scores[d, rows, :] = factor * x
        if d in (0, 3):
            @pl.when(xh == (1 if d == 0 else 0))
            def _():
                scores[d, rows, pl.ds(R, R)] = jnp.full((x.shape[0], R), LOW, F32)

        return chunk_stats(scores.at[d], col_part.at[d], start, x.shape[0])

    state = keep_scores(0, 0, dot_t(texts[0], images[pl.ds(0, 2 * R), :]))
    col_part[0] = tile_of(*merge([pair_of(col_part[0]), pair_of(col_diag[...])]))
    for c in range(NC):
        arrived(1, 1, c)
        arrived(3, 0, c)
        arrived(2, 0, c)
        arrived(2, 1, c)
        rows = pl.ds(c * CH, CH)
        joined = jnp.concatenate([texts[d, rows, :] for d in (1, 2, 3)], axis=0)
        x = dot_t(joined, images[pl.ds(0, 2 * R), :])
        state = merge([state] + [keep_scores(d, c * CH, x[(d - 1) * CH:d * CH, :]) for d in (1, 2, 3)])

    both = tile_of(*state)
    row_part[0] = both[:, 0:R]
    row_part[1] = both[:, R:2 * R]
    sends = []
    steps = (1, 2, 3, -1, -2, -3)
    for k, step in enumerate(steps):
        low, high = max(0, -step), min(4, 4 - step)
        sends.append(rcopy(
            col_part.at[pl.ds(low, high - low)],
            col_peer.at[k, pl.ds(low + step, high - low)],
            col_ss.at[k], col_rs.at[k], at_row(step),
        ))
    sends.append(rcopy(row_part, row_peer, row_ss.at[0], row_rs.at[0], peer))
    sends.append(rcopy(row_part.at[0], row_back.at[0], row_ss.at[1], row_rs.at[1], owner_same))
    sends.append(rcopy(row_part.at[1], row_back.at[1], row_ss.at[2], row_rs.at[2], owner_other))
    sends.append(rcopy(row_diag, row_owner.at[0], row_ss.at[3], row_rs.at[3], handler_same))
    sends.append(rcopy(row_diag, row_owner.at[1], row_ss.at[4], row_rs.at[4], handler_other))
    for copy in sends:
        copy.start()
    for copy in sends:
        copy.wait_recv()

    def far_mate(k):
        place = (big_y // 4 * 2 + xh + k) % 8
        return (group, (place // 2 * 4 + y) * 2 + place % 2)

    stages = [
        (group, 4, lambda k: ((group + k) % 4, same)),
        (y, 4, lambda k: (group, (big_y - y + (y + k) % 4) * 2 + xh)),
        (big_y // 4 * 2 + xh, 8, far_mate),
    ]

    def loss_copy(stage, k):
        place, _, mate = stages[stage]
        return rcopy(
            loss_out.at[stage], loss_in.at[stage, place],
            loss_ss.at[stage, k], loss_rs.at[stage, place], mate(k),
        )

    def loss_send(stage, value):
        place, count, _ = stages[stage]
        loss_out[stage] = value
        loss_in[stage, place] = value
        for k in range(1, count):
            loss_copy(stage, k).start()

    def loss_sum(stage):
        place, count, _ = stages[stage]
        for k in range(1, count):
            other_place = (place + k) % count
            rcopy(
                loss_out.at[stage], loss_in.at[stage, other_place],
                loss_ss.at[stage, k], loss_rs.at[stage, other_place], peer,
            ).wait_recv()
        return sum(loss_in[stage, i] for i in range(count))

    def lse(parts):
        peak, total = merge(parts)
        return peak + jnp.log(total)

    row_lse = jnp.concatenate(
        [lse([pair_of(row_part[k]), pair_of(row_peer[1 - k]), pair_of(row_owner[k])]) for k in range(2)],
        axis=1,
    )
    own_row_lse = lse([pair_of(row_diag[...]), pair_of(row_back[0]), pair_of(row_back[1])])

    def col_lse(d):
        parts = [pair_of(col_part[d])]
        for k, step in enumerate(steps):
            if 0 <= d - step <= 3:
                parts.append(pair_of(col_peer[k, d]))
        value = lse(parts)
        col_column[d] = jnp.transpose(jnp.broadcast_to(value, (128, R)))
        return value

    def block_weights(d):
        for c in range(2):
            rows = pl.ds(c * (R // 2), R // 2)
            x = scores[d, rows, :]
            col = jnp.concatenate([col_column[d, rows, :]] * (2 * R // 128), axis=1)
            weights[d, rows, pl.ds(0, 2 * R)] = (jnp.exp(x - row_lse) + jnp.exp(x - col)).astype(BF16)

    def text_part(d, half):
        return dot_n(weights[d, :, pl.ds(0, 2 * R)], images[pl.ds(0, 2 * R), pl.ds(half * H, H)])

    def flip(d):
        weights_t[:, pl.ds(d * R, R)] = jnp.transpose(weights[d, :, pl.ds(0, 2 * R)])

    wrap_down = 1 - (y + 3) // 4
    down_slot = 2 * wrap_down
    down_far = at_row(-1 - 3 * wrap_down)
    back_far = at_row(-3)

    def cut(ref, half, c):
        return ref.at[pl.ds(c * CH, CH), pl.ds(half * H, H)]

    def half_copy(half, c, dev):
        return rcopy(
            cut(part2, half, c), half_in.at[half, pl.ds(c * CH, CH)],
            half_ss.at[half, c], half_rs.at[half, c], dev,
        )

    def part_copy(ref, stream, slot, half, c, dev):
        return rcopy(
            cut(ref, half, c), part_of(part_in, slot, half, c),
            part_ss.at[stream, half, c], part_rs.at[slot, half, c], dev,
        )

    def part_arrived(slot, half, c):
        ref = part_of(part_in, slot, half, c)
        rcopy(ref, ref, part_ss.at[0, half, c], part_rs.at[slot, half, c], up).wait_recv()

    def back_copy(half, c):
        return rcopy(
            part_of(part_in, 2, half, c), part_of(part_in, 0, half, c),
            back_ss.at[half, c], part_rs.at[0, half, c], at_row(3),
        )

    col_lse(2)
    block_weights(2)
    part2[:, pl.ds(0, H)] = text_part(2, 0).astype(BF16)
    for c in range(NC):
        half_copy(0, c, down).start()
    part2[:, pl.ds(H, H)] = text_part(2, 1).astype(BF16)
    for c in range(NC):
        half_copy(1, c, up).start()
    own_col_lse = col_lse(0)
    terms = jnp.sum(own_row_lse) + jnp.sum(own_col_lse) - 2.0 * chosen
    loss_send(0, jnp.full((8, 128), terms, F32))
    col_lse(1)
    block_weights(1)
    part1[:, pl.ds(H, H)] = text_part(1, 1).astype(BF16)
    for c in range(NC):
        part_copy(part1, 0, down_slot, 1, c, down_far).start()
    col_lse(3)
    block_weights(3)
    part3[:, pl.ds(0, H)] = text_part(3, 0).astype(BF16)
    for c in range(NC):
        part_copy(part3, 1, 1, 0, c, back_far).start()
    stash1[...] = text_part(1, 0)
    stash3[...] = text_part(3, 1)

    def image_part(k):
        flat = texts.reshape(5 * R, D)[pl.ds(0, 4 * R), :]
        grad_send[k] = dot_n(weights_t[pl.ds(k * R, R), :], flat).astype(BF16)

    grad_other = rcopy(grad_send.at[1], grad_in.at[1], grad_ss.at[1], grad_rs.at[1], owner_other)
    grad_same = rcopy(grad_send.at[0], grad_in.at[0], grad_ss.at[0], grad_rs.at[0], owner_same)
    def add_halves(c):
        rows = pl.ds(c * CH, CH)
        half_copy(0, c, down).wait_recv()
        part1[rows, pl.ds(0, H)] = (stash1[rows, :] + half_in[0, rows, :].astype(F32)).astype(BF16)
        part_copy(part1, 0, down_slot, 0, c, down_far).start()
        half_copy(1, c, up).wait_recv()
        part3[rows, pl.ds(H, H)] = (stash3[rows, :] + half_in[1, rows, :].astype(F32)).astype(BF16)
        part_copy(part3, 1, 1, 1, c, back_far).start()

    def relay_parts(half):
        @pl.when(y == 0)
        def _():
            for c in range(NC):
                part_arrived(2, half, c)
                back_copy(half, c).start()

    add_halves(0)
    block_weights(0)
    for d in range(4):
        flip(d)
    image_part(1)
    grad_other.start()
    loss_send(1, loss_sum(0))
    add_halves(1)
    image_part(0)
    grad_same.start()
    add_halves(2)
    relay_parts(1)
    loss_send(2, loss_sum(1))

    x = own_scores[...]
    own_col = jnp.concatenate([col_column[0]] * (R // 128), axis=1)
    own_w = jnp.exp(x - own_row_lse) + jnp.exp(x - own_col)
    weights[0, :, pl.ds(2 * R, R)] = jnp.where(mask, own_w - 2.0, own_w).astype(BF16)
    own_weights_t[...] = jnp.transpose(weights[0, :, pl.ds(2 * R, R)])
    relay_parts(0)

    text_acc[...] = dot_n(weights[0], images[...])
    image_acc[...] = dot_n(own_weights_t[...], texts[0])


    grad_other.wait_recv()
    grad_same.wait_recv()

    def out_copy(acc, out, k, c):
        rows = pl.ds(pl.multiple_of(c * CH, CH), CH)
        return pltpu.make_async_copy(acc.at[rows], out.at[rows], local_sem.at[2 + k * NC + c])

    def finish_image(c, _):
        rows = pl.ds(pl.multiple_of(c * CH, CH), CH)
        image_acc[rows, :] = factor * (
            image_acc[rows, :] + grad_in[0, rows, :].astype(F32) + grad_in[1, rows, :].astype(F32)
        )
        out_copy(image_acc, image_out, 0, c).start()
        return 0

    lax.fori_loop(0, NC, finish_image, 0)

    def finish_text(c, _):
        rows = pl.ds(pl.multiple_of(c * CH, CH), CH)
        for slot in range(2):
            for half in range(2):
                part_arrived(slot, half, c)
        text_acc[rows, :] = factor * (
            text_acc[rows, :] + part_in[0, rows, :].astype(F32) + part_in[1, rows, :].astype(F32)
        )
        out_copy(text_acc, text_out, 1, c).start()
        return 0

    lax.fori_loop(0, NC, finish_text, 0)

    to_other.wait_send()
    to_same.wait_send()
    for copy in sends:
        copy.wait_send()
    grad_other.wait_send()
    grad_same.wait_send()
    for stage, (_, count, _) in enumerate(stages):
        for k in range(1, count):
            loss_copy(stage, k).wait_send()
    loss_ref[0] = loss_sum(2)[0, 0] * (0.5 / (R * 128))

    def drain(c, _):
        own_copy(0, up_slot, 0, c, up_far).wait_send()
        own_copy(1, 3, 1, c, far).wait_send()
        own_copy(2, up_slot, 1, c, up_far).wait_send()
        own_copy(3, 3, 0, c, far).wait_send()
        fwd_copy(0, 1, 0, c, up).wait_send()
        fwd_copy(1, 3, 1, c, down).wait_send()
        half_copy(0, c, down).wait_send()
        half_copy(1, c, up).wait_send()
        for half in range(2):
            part_copy(part1, 0, down_slot, half, c, down_far).wait_send()
            part_copy(part3, 1, 1, half, c, back_far).wait_send()

        @pl.when(y == 3)
        def _():
            relay_copy(0, c).wait_send()
            relay_copy(1, c).wait_send()

        @pl.when(y == 0)
        def _():
            back_copy(0, c).wait_send()
            back_copy(1, c).wait_send()

        out_copy(image_acc, image_out, 0, c).wait()
        out_copy(text_acc, text_out, 1, c).wait()
        return 0

    lax.fori_loop(0, NC, drain, 0)


def on_device(image_emb, text_emb, positive, logit_scale):
    vmem, dma = pltpu.VMEM, pltpu.SemaphoreType.DMA
    return pl.pallas_call(
        kernel,
        out_shape=(
            jax.ShapeDtypeStruct((1,), F32),
            jax.ShapeDtypeStruct((R, D), F32),
            jax.ShapeDtypeStruct((R, D), F32),
        ),
        in_specs=[
            pl.BlockSpec(memory_space=pltpu.SMEM),
            pl.BlockSpec(memory_space=pltpu.HBM),
            pl.BlockSpec(memory_space=pltpu.HBM),
            pl.BlockSpec(memory_space=pltpu.HBM),
        ],
        out_specs=(
            pl.BlockSpec(memory_space=pltpu.SMEM),
            pl.BlockSpec(memory_space=pl.ANY),
            pl.BlockSpec(memory_space=pl.ANY),
        ),
        scratch_shapes=[
            vmem((5, R, D), BF16),
            vmem((3 * R, D), BF16),
            vmem((4, R, 2 * R), F32),
            vmem((R, R), F32),
            vmem((4, R, 3 * R), BF16),
            vmem((2 * R, 4 * R), BF16),
            vmem((R, R), BF16),
            vmem((4, R, 128), F32),
            vmem((2, 8, R), F32),
            vmem((8, R), F32),
            vmem((4, 8, R), F32),
            vmem((8, R), F32),
            vmem((2, 8, R), F32),
            vmem((2, 8, R), F32),
            vmem((2, 8, R), F32),
            vmem((6, 4, 8, R), F32),
            vmem((R, D), BF16),
            vmem((R, D), BF16),
            vmem((R, D), BF16),
            vmem((R, H), F32),
            vmem((R, H), F32),
            vmem((3, R, D), BF16),
            vmem((2, R, H), BF16),
            vmem((2, R, D), BF16),
            vmem((2, R, D), BF16),
            vmem((R, D), F32),
            vmem((R, D), F32),
            dma((3 + 2 * NC,)),
            dma((4, NC)),
            dma((5, 2, NC)),
            dma((2, NC)),
            dma((2, NC)),
            dma((2,)),
            dma((2,)),
            dma((5,)),
            dma((5,)),
            dma((6,)),
            dma((6,)),
            dma((2, NC)),
            dma((2, NC)),
            dma((2, 2, NC)),
            dma((3, 2, NC)),
            dma((2, NC)),
            dma((2,)),
            dma((2,)),
            vmem((3, 8, 128), F32),
            vmem((3, 8, 8, 128), F32),
            dma((3, 8)),
            dma((3, 8)),
            vmem((R,), jnp.int32),
        ],
        compiler_params=pltpu.CompilerParams(
            collective_id=0, has_side_effects=True, vmem_limit_bytes=54 * 1024 * 1024
        ),
    )(logit_scale, image_emb, text_emb, positive)


def solution(mesh):
    placed = (P(("group", "blk"), None), P(("group", "blk"), None), P(("group", "blk")), P())
    return jax.shard_map(
        on_device,
        mesh=mesh,
        in_specs=placed,
        out_specs=(P(), P(("group", "blk"), None), P(("group", "blk"), None)),
        check_vma=False,
    )
```

```python
import functools

import jax
import jax.numpy as jnp
from jax import lax
from jax.experimental import pallas as pl
from jax.experimental.pallas import tpu as pltpu
from jax.sharding import PartitionSpec as P

MESH = pl.DeviceIdType.MESH
F32 = jnp.float32
BF16 = jnp.bfloat16
R = 384
D = 1280
H = D // 2
NC = 3
CH = R // NC
LOW = -1e30
RING = 16


def rcopy(src, dst, ss, rs, dev):
    return pltpu.make_async_remote_copy(
        src_ref=src, dst_ref=dst, send_sem=ss, recv_sem=rs, device_id=dev, device_id_type=MESH
    )


def dot_t(a, b):
    return lax.dot_general(a, b, (((1,), (1,)), ((), ())), preferred_element_type=F32)


def dot_n(a, b):
    return lax.dot_general(a, b, (((1,), (0,)), ((), ())), preferred_element_type=F32)


def merge(parts):
    peak = functools.reduce(jnp.maximum, [m for m, _ in parts])
    total = sum(s * jnp.exp(m - peak) for m, s in parts)
    return peak, total


def tile_of(peak, total):
    row = lax.broadcasted_iota(jnp.int32, (8, peak.shape[1]), 0)
    return jnp.where(row == 0, peak, total)


def pair_of(tile):
    return tile[0:1, :], tile[1:2, :]


def kernel(
    scale_ref, image_ref, text_ref, pos_ref,
    loss_ref, image_out, text_out,
    texts, images, scores, own_scores, weights, weights_t, own_weights_t,
    col_column, row_part, row_diag, col_part, col_diag,
    row_peer, row_owner, row_back, col_peer,
    part1, part2, part3, stash1, stash3, part_in, half_in,
    grad_send, grad_in, image_acc, text_acc,
    local_sem, fetch_ss, fetch_rs, fwd_ss, relay_ss, img_ss, img_rs,
    row_ss, row_rs, col_ss, col_rs,
    half_ss, half_rs, part_ss, part_rs, back_ss, grad_ss, grad_rs,
    loss_out, loss_in, loss_ss, loss_rs, pos_vmem,
):
    group = lax.axis_index("group")
    blk = lax.axis_index("blk")
    xh = blk % 2
    big_y = blk // 2
    y = big_y % 4
    factor = scale_ref[0]

    def at_row(step):
        return (group, ((big_y + step + RING) % RING) * 2 + xh)

    up, down = at_row(1), at_row(-1)
    behind = (group + 3) % 4
    ahead = (group + 1) % 4
    same, other = blk, big_y * 2 + (1 - xh)
    handler_same, handler_other = (behind, same), (behind, other)
    owner_same, owner_other = (ahead, same), (ahead, other)
    peer = (group, other)

    text_copy = pltpu.make_async_copy(text_ref, texts.at[0], local_sem.at[0])
    image_copy = pltpu.make_async_copy(image_ref, images.at[pl.ds(2 * R, R)], local_sem.at[1])
    pos_copy = pltpu.make_async_copy(pos_ref, pos_vmem, local_sem.at[2 + 2 * NC])
    text_copy.start()
    pos_copy.start()
    image_copy.start()

    barrier = pltpu.get_barrier_semaphore()
    partners = [at_row(step) for step in range(1, RING)]
    partners += [((group + k) % 4, blk) for k in (1, 2, 3)]
    partners += [((group + k) % 4, other) for k in range(4)]
    for dev in partners:
        pl.semaphore_signal(barrier, inc=1, device_id=dev, device_id_type=MESH)
    pl.semaphore_wait(barrier, len(partners))

    def part_of(ref, slot, half, c):
        return ref.at[slot, pl.ds(c * CH, CH), pl.ds(half * H, H)]

    wrap_up = y // 3
    up_slot = 1 + 3 * wrap_up
    up_far = at_row(1 + 3 * wrap_up)
    far = at_row(3)

    def own_copy(stream, slot, half, c, dev):
        return rcopy(
            part_of(texts, 0, half, c), part_of(texts, slot, half, c),
            fetch_ss.at[stream, c], fetch_rs.at[slot, half, c], dev,
        )

    def arrived(slot, half, c):
        ref = part_of(texts, slot, half, c)
        rcopy(ref, ref, fetch_ss.at[0, c], fetch_rs.at[slot, half, c], up).wait_recv()

    def fwd_copy(stream, slot, half, c, dev):
        return rcopy(
            part_of(texts, slot, half, c), part_of(texts, 2, half, c),
            fwd_ss.at[stream, c], fetch_rs.at[2, half, c], dev,
        )

    def relay_copy(half, c):
        return rcopy(
            part_of(texts, 4, half, c), part_of(texts, 1, half, c),
            relay_ss.at[half, c], fetch_rs.at[1, half, c], at_row(-3),
        )

    text_copy.wait()
    for c in range(NC):
        own_copy(0, up_slot, 0, c, up_far).start()
        own_copy(1, 3, 1, c, far).start()
    image_copy.wait()
    own_image = images.at[pl.ds(2 * R, R)]
    to_other = rcopy(own_image, images.at[pl.ds(R, R)], img_ss.at[1], img_rs.at[1], handler_other)
    to_same = rcopy(own_image, images.at[pl.ds(0, R)], img_ss.at[0], img_rs.at[0], handler_same)
    to_other.start()
    to_same.start()

    def chunk_stats(ref, cols_ref, start, size):
        rows = pl.ds(start, size)
        lane = lax.broadcasted_iota(jnp.int32, (size, 128), 1)
        x = ref[rows, :]
        peak = jnp.max(x, axis=1, keepdims=True)
        total = jnp.sum(jnp.exp(x - peak), axis=1, keepdims=True)
        cols_ref[:, rows] = jnp.transpose(jnp.where(lane == 0, peak, total))[0:8, :]
        row_peak = jnp.max(x, axis=0, keepdims=True)
        return row_peak, jnp.sum(jnp.exp(x - row_peak), axis=0, keepdims=True)

    own_scores[...] = factor * dot_t(texts[0], images[pl.ds(2 * R, R), :])
    pos_copy.wait()
    positive = pos_vmem[...].reshape(1, R)
    mask = lax.broadcasted_iota(jnp.int32, (R, R), 0) == positive
    chosen = jnp.sum(jnp.where(mask, own_scores[...], 0.0))
    row_diag[...] = tile_of(*chunk_stats(own_scores, col_diag, 0, R))

    def forward(c, _):
        @pl.when(y == 3)
        def _():
            arrived(4, 0, c)
            relay_copy(0, c).start()

        arrived(1, 0, c)
        fwd_copy(0, 1, 0, c, up).start()
        arrived(3, 1, c)
        fwd_copy(1, 3, 1, c, down).start()
        own_copy(2, up_slot, 1, c, up_far).start()
        own_copy(3, 3, 0, c, far).start()
        return 0

    lax.fori_loop(0, NC, forward, 0)

    @pl.when(y == 3)
    def _():
        def relay(c, _):
            arrived(4, 1, c)
            relay_copy(1, c).start()
            return 0

        lax.fori_loop(0, NC, relay, 0)

    to_other.wait_recv()
    to_same.wait_recv()

    def keep_scores(d, start, x):
        rows = pl.ds(start, x.shape[0])
        scores[d, rows, :] = factor * x
        if d in (0, 3):
            @pl.when(xh == (1 if d == 0 else 0))
            def _():
                scores[d, rows, pl.ds(R, R)] = jnp.full((x.shape[0], R), LOW, F32)

        return chunk_stats(scores.at[d], col_part.at[d], start, x.shape[0])

    state = keep_scores(0, 0, dot_t(texts[0], images[pl.ds(0, 2 * R), :]))
    col_part[0] = tile_of(*merge([pair_of(col_part[0]), pair_of(col_diag[...])]))
    for c in range(NC):
        arrived(1, 1, c)
        arrived(3, 0, c)
        arrived(2, 0, c)
        arrived(2, 1, c)
        rows = pl.ds(c * CH, CH)
        joined = jnp.concatenate([texts[d, rows, :] for d in (1, 2, 3)], axis=0)
        x = dot_t(joined, images[pl.ds(0, 2 * R), :])
        state = merge([state] + [keep_scores(d, c * CH, x[(d - 1) * CH:d * CH, :]) for d in (1, 2, 3)])

    both = tile_of(*state)
    row_part[0] = both[:, 0:R]
    row_part[1] = both[:, R:2 * R]
    sends = []
    steps = (1, 2, 3, -1, -2, -3)
    for k, step in enumerate(steps):
        low, high = max(0, -step), min(4, 4 - step)
        sends.append(rcopy(
            col_part.at[pl.ds(low, high - low)],
            col_peer.at[k, pl.ds(low + step, high - low)],
            col_ss.at[k], col_rs.at[k], at_row(step),
        ))
    sends.append(rcopy(row_part, row_peer, row_ss.at[0], row_rs.at[0], peer))
    sends.append(rcopy(row_part.at[0], row_back.at[0], row_ss.at[1], row_rs.at[1], owner_same))
    sends.append(rcopy(row_part.at[1], row_back.at[1], row_ss.at[2], row_rs.at[2], owner_other))
    sends.append(rcopy(row_diag, row_owner.at[0], row_ss.at[3], row_rs.at[3], handler_same))
    sends.append(rcopy(row_diag, row_owner.at[1], row_ss.at[4], row_rs.at[4], handler_other))
    for copy in sends:
        copy.start()
    for copy in sends:
        copy.wait_recv()

    def near_mate(k):
        place = (group * 2 + xh + k) % 8
        return (place // 2, big_y * 2 + place % 2)

    stages = [(group * 2 + xh, 8, near_mate), (big_y, RING, at_row)]

    def loss_copy(stage, k):
        place, _, mate = stages[stage]
        return rcopy(
            loss_out.at[stage], loss_in.at[stage, place],
            loss_ss.at[stage, k], loss_rs.at[stage, place], mate(k),
        )

    def loss_send(stage, value):
        place, count, _ = stages[stage]
        loss_out[stage] = value
        loss_in[stage, place] = value
        for k in range(1, count):
            loss_copy(stage, k).start()

    def loss_sum(stage):
        place, count, _ = stages[stage]
        for k in range(1, count):
            other_place = (place + k) % count
            rcopy(
                loss_out.at[stage], loss_in.at[stage, other_place],
                loss_ss.at[stage, k], loss_rs.at[stage, other_place], peer,
            ).wait_recv()
        return sum(loss_in[stage, i] for i in range(count))

    def lse(parts):
        peak, total = merge(parts)
        return peak + jnp.log(total)

    row_lse = jnp.concatenate(
        [lse([pair_of(row_part[k]), pair_of(row_peer[1 - k]), pair_of(row_owner[k])]) for k in range(2)],
        axis=1,
    )
    own_row_lse = lse([pair_of(row_diag[...]), pair_of(row_back[0]), pair_of(row_back[1])])

    def col_lse(d):
        parts = [pair_of(col_part[d])]
        for k, step in enumerate(steps):
            if 0 <= d - step <= 3:
                parts.append(pair_of(col_peer[k, d]))
        value = lse(parts)
        col_column[d] = jnp.transpose(jnp.broadcast_to(value, (128, R)))
        return value

    def block_weights(d):
        for c in range(2):
            rows = pl.ds(c * (R // 2), R // 2)
            x = scores[d, rows, :]
            col = jnp.concatenate([col_column[d, rows, :]] * (2 * R // 128), axis=1)
            weights[d, rows, pl.ds(0, 2 * R)] = (jnp.exp(x - row_lse) + jnp.exp(x - col)).astype(BF16)

    def text_part(d, half):
        return dot_n(weights[d, :, pl.ds(0, 2 * R)], images[pl.ds(0, 2 * R), pl.ds(half * H, H)])

    def flip(d):
        weights_t[:, pl.ds(d * R, R)] = jnp.transpose(weights[d, :, pl.ds(0, 2 * R)])

    wrap_down = 1 - (y + 3) // 4
    down_slot = 2 * wrap_down
    down_far = at_row(-1 - 3 * wrap_down)
    back_far = at_row(-3)

    def cut(ref, half, c):
        return ref.at[pl.ds(c * CH, CH), pl.ds(half * H, H)]

    def half_copy(half, c, dev):
        return rcopy(
            cut(part2, half, c), half_in.at[half, pl.ds(c * CH, CH)],
            half_ss.at[half, c], half_rs.at[half, c], dev,
        )

    def part_copy(ref, stream, slot, half, c, dev):
        return rcopy(
            cut(ref, half, c), part_of(part_in, slot, half, c),
            part_ss.at[stream, half, c], part_rs.at[slot, half, c], dev,
        )

    def part_arrived(slot, half, c):
        ref = part_of(part_in, slot, half, c)
        rcopy(ref, ref, part_ss.at[0, half, c], part_rs.at[slot, half, c], up).wait_recv()

    def back_copy(half, c):
        return rcopy(
            part_of(part_in, 2, half, c), part_of(part_in, 0, half, c),
            back_ss.at[half, c], part_rs.at[0, half, c], at_row(3),
        )

    col_lse(2)
    block_weights(2)
    part2[:, pl.ds(0, H)] = text_part(2, 0).astype(BF16)
    for c in range(NC):
        half_copy(0, c, down).start()
    part2[:, pl.ds(H, H)] = text_part(2, 1).astype(BF16)
    for c in range(NC):
        half_copy(1, c, up).start()
    own_col_lse = col_lse(0)
    terms = jnp.sum(own_row_lse) + jnp.sum(own_col_lse) - 2.0 * chosen
    loss_send(0, jnp.full((8, 128), terms, F32))
    col_lse(1)
    block_weights(1)
    part1[:, pl.ds(H, H)] = text_part(1, 1).astype(BF16)
    for c in range(NC):
        part_copy(part1, 0, down_slot, 1, c, down_far).start()
    loss_send(1, loss_sum(0))
    col_lse(3)
    block_weights(3)
    part3[:, pl.ds(0, H)] = text_part(3, 0).astype(BF16)
    for c in range(NC):
        part_copy(part3, 1, 1, 0, c, back_far).start()
    stash1[...] = text_part(1, 0)
    stash3[...] = text_part(3, 1)

    def image_part(k):
        flat = texts.reshape(5 * R, D)[pl.ds(0, 4 * R), :]
        grad_send[k] = dot_n(weights_t[pl.ds(k * R, R), :], flat).astype(BF16)

    grad_other = rcopy(grad_send.at[1], grad_in.at[1], grad_ss.at[1], grad_rs.at[1], owner_other)
    grad_same = rcopy(grad_send.at[0], grad_in.at[0], grad_ss.at[0], grad_rs.at[0], owner_same)
    def add_halves(c):
        rows = pl.ds(c * CH, CH)
        half_copy(0, c, down).wait_recv()
        part1[rows, pl.ds(0, H)] = (stash1[rows, :] + half_in[0, rows, :].astype(F32)).astype(BF16)
        part_copy(part1, 0, down_slot, 0, c, down_far).start()
        half_copy(1, c, up).wait_recv()
        part3[rows, pl.ds(H, H)] = (stash3[rows, :] + half_in[1, rows, :].astype(F32)).astype(BF16)
        part_copy(part3, 1, 1, 1, c, back_far).start()

    def relay_parts(half):
        @pl.when(y == 0)
        def _():
            for c in range(NC):
                part_arrived(2, half, c)
                back_copy(half, c).start()

    add_halves(0)
    block_weights(0)
    for d in range(4):
        flip(d)
    image_part(1)
    grad_other.start()
    add_halves(1)
    image_part(0)
    grad_same.start()
    add_halves(2)
    relay_parts(1)

    x = own_scores[...]
    own_col = jnp.concatenate([col_column[0]] * (R // 128), axis=1)
    own_w = jnp.exp(x - own_row_lse) + jnp.exp(x - own_col)
    weights[0, :, pl.ds(2 * R, R)] = jnp.where(mask, own_w - 2.0, own_w).astype(BF16)
    own_weights_t[...] = jnp.transpose(weights[0, :, pl.ds(2 * R, R)])
    relay_parts(0)

    text_acc[...] = dot_n(weights[0], images[...])
    image_acc[...] = dot_n(own_weights_t[...], texts[0])


    grad_other.wait_recv()
    grad_same.wait_recv()

    def out_copy(acc, out, k, c):
        rows = pl.ds(pl.multiple_of(c * CH, CH), CH)
        return pltpu.make_async_copy(acc.at[rows], out.at[rows], local_sem.at[2 + k * NC + c])

    def finish_image(c, _):
        rows = pl.ds(pl.multiple_of(c * CH, CH), CH)
        image_acc[rows, :] = factor * (
            image_acc[rows, :] + grad_in[0, rows, :].astype(F32) + grad_in[1, rows, :].astype(F32)
        )
        out_copy(image_acc, image_out, 0, c).start()
        return 0

    lax.fori_loop(0, NC, finish_image, 0)

    def finish_text(c, _):
        rows = pl.ds(pl.multiple_of(c * CH, CH), CH)
        for slot in range(2):
            for half in range(2):
                part_arrived(slot, half, c)
        text_acc[rows, :] = factor * (
            text_acc[rows, :] + part_in[0, rows, :].astype(F32) + part_in[1, rows, :].astype(F32)
        )
        out_copy(text_acc, text_out, 1, c).start()
        return 0

    lax.fori_loop(0, NC, finish_text, 0)

    to_other.wait_send()
    to_same.wait_send()
    for copy in sends:
        copy.wait_send()
    grad_other.wait_send()
    grad_same.wait_send()
    for stage, (_, count, _) in enumerate(stages):
        for k in range(1, count):
            loss_copy(stage, k).wait_send()
    loss_ref[0] = loss_sum(1)[0, 0] * (0.5 / (R * 128))

    def drain(c, _):
        own_copy(0, up_slot, 0, c, up_far).wait_send()
        own_copy(1, 3, 1, c, far).wait_send()
        own_copy(2, up_slot, 1, c, up_far).wait_send()
        own_copy(3, 3, 0, c, far).wait_send()
        fwd_copy(0, 1, 0, c, up).wait_send()
        fwd_copy(1, 3, 1, c, down).wait_send()
        half_copy(0, c, down).wait_send()
        half_copy(1, c, up).wait_send()
        for half in range(2):
            part_copy(part1, 0, down_slot, half, c, down_far).wait_send()
            part_copy(part3, 1, 1, half, c, back_far).wait_send()

        @pl.when(y == 3)
        def _():
            relay_copy(0, c).wait_send()
            relay_copy(1, c).wait_send()

        @pl.when(y == 0)
        def _():
            back_copy(0, c).wait_send()
            back_copy(1, c).wait_send()

        out_copy(image_acc, image_out, 0, c).wait()
        out_copy(text_acc, text_out, 1, c).wait()
        return 0

    lax.fori_loop(0, NC, drain, 0)


def on_device(image_emb, text_emb, positive, logit_scale):
    vmem, dma = pltpu.VMEM, pltpu.SemaphoreType.DMA
    return pl.pallas_call(
        kernel,
        out_shape=(
            jax.ShapeDtypeStruct((1,), F32),
            jax.ShapeDtypeStruct((R, D), F32),
            jax.ShapeDtypeStruct((R, D), F32),
        ),
        in_specs=[
            pl.BlockSpec(memory_space=pltpu.SMEM),
            pl.BlockSpec(memory_space=pltpu.HBM),
            pl.BlockSpec(memory_space=pltpu.HBM),
            pl.BlockSpec(memory_space=pltpu.HBM),
        ],
        out_specs=(
            pl.BlockSpec(memory_space=pltpu.SMEM),
            pl.BlockSpec(memory_space=pl.ANY),
            pl.BlockSpec(memory_space=pl.ANY),
        ),
        scratch_shapes=[
            vmem((5, R, D), BF16),
            vmem((3 * R, D), BF16),
            vmem((4, R, 2 * R), F32),
            vmem((R, R), F32),
            vmem((4, R, 3 * R), BF16),
            vmem((2 * R, 4 * R), BF16),
            vmem((R, R), BF16),
            vmem((4, R, 128), F32),
            vmem((2, 8, R), F32),
            vmem((8, R), F32),
            vmem((4, 8, R), F32),
            vmem((8, R), F32),
            vmem((2, 8, R), F32),
            vmem((2, 8, R), F32),
            vmem((2, 8, R), F32),
            vmem((6, 4, 8, R), F32),
            vmem((R, D), BF16),
            vmem((R, D), BF16),
            vmem((R, D), BF16),
            vmem((R, H), F32),
            vmem((R, H), F32),
            vmem((3, R, D), BF16),
            vmem((2, R, H), BF16),
            vmem((2, R, D), BF16),
            vmem((2, R, D), BF16),
            vmem((R, D), F32),
            vmem((R, D), F32),
            dma((3 + 2 * NC,)),
            dma((4, NC)),
            dma((5, 2, NC)),
            dma((2, NC)),
            dma((2, NC)),
            dma((2,)),
            dma((2,)),
            dma((5,)),
            dma((5,)),
            dma((6,)),
            dma((6,)),
            dma((2, NC)),
            dma((2, NC)),
            dma((2, 2, NC)),
            dma((3, 2, NC)),
            dma((2, NC)),
            dma((2,)),
            dma((2,)),
            vmem((2, 8, 128), F32),
            vmem((2, RING, 8, 128), F32),
            dma((2, RING)),
            dma((2, RING)),
            vmem((R,), jnp.int32),
        ],
        compiler_params=pltpu.CompilerParams(
            collective_id=0, has_side_effects=True, vmem_limit_bytes=54 * 1024 * 1024
        ),
    )(logit_scale, image_emb, text_emb, positive)


def solution(mesh):
    placed = (P(("group", "blk"), None), P(("group", "blk"), None), P(("group", "blk")), P())
    return jax.shard_map(
        on_device,
        mesh=mesh,
        in_specs=placed,
        out_specs=(P(), P(("group", "blk"), None), P(("group", "blk"), None)),
        check_vma=False,
    )
```

```python
import functools

import jax
import jax.numpy as jnp
from jax import lax
from jax.experimental import pallas as pl
from jax.experimental.pallas import tpu as pltpu
from jax.sharding import PartitionSpec as P

MESH = pl.DeviceIdType.MESH
F32 = jnp.float32
BF16 = jnp.bfloat16
R = 384
D = 1280
H = D // 2
NC = 3
CH = R // NC
LOW = -1e30
RING = 16


def rcopy(src, dst, ss, rs, dev):
    return pltpu.make_async_remote_copy(
        src_ref=src, dst_ref=dst, send_sem=ss, recv_sem=rs, device_id=dev, device_id_type=MESH
    )


def dot_t(a, b):
    return lax.dot_general(a, b, (((1,), (1,)), ((), ())), preferred_element_type=F32)


def dot_n(a, b):
    return lax.dot_general(a, b, (((1,), (0,)), ((), ())), preferred_element_type=F32)


def merge(parts):
    peak = functools.reduce(jnp.maximum, [m for m, _ in parts])
    total = sum(s * jnp.exp(m - peak) for m, s in parts)
    return peak, total


def tile_of(peak, total):
    row = lax.broadcasted_iota(jnp.int32, (8, peak.shape[1]), 0)
    return jnp.where(row == 0, peak, total)


def pair_of(tile):
    return tile[0:1, :], tile[1:2, :]


def kernel(
    scale_ref, image_ref, text_ref, pos_ref,
    loss_ref, image_out, text_out,
    texts, images, scores, own_scores, weights, weights_t, own_weights_t,
    col_column, row_part, row_diag, col_part, col_diag,
    row_peer, row_owner, row_back, col_peer,
    part1, part2, part3, stash1, stash3, part_in, half_in,
    grad_send, grad_in,
    local_sem, fetch_ss, fetch_rs, fwd_ss, relay_ss, img_ss, img_rs,
    row_ss, row_rs, col_ss, col_rs,
    half_ss, half_rs, part_ss, part_rs, back_ss, grad_ss, grad_rs,
    loss_out, loss_in, loss_ss, loss_rs, pos_vmem,
):
    group = lax.axis_index("group")
    blk = lax.axis_index("blk")
    xh = blk % 2
    big_y = blk // 2
    y = big_y % 4
    factor = scale_ref[0]

    def at_row(step):
        return (group, ((big_y + step + RING) % RING) * 2 + xh)

    up, down = at_row(1), at_row(-1)
    behind = (group + 3) % 4
    ahead = (group + 1) % 4
    same, other = blk, big_y * 2 + (1 - xh)
    handler_same, handler_other = (behind, same), (behind, other)
    owner_same, owner_other = (ahead, same), (ahead, other)
    peer = (group, other)

    text_copy = pltpu.make_async_copy(text_ref, texts.at[0], local_sem.at[0])
    image_copy = pltpu.make_async_copy(image_ref, images.at[pl.ds(2 * R, R)], local_sem.at[1])
    pos_copy = pltpu.make_async_copy(pos_ref, pos_vmem, local_sem.at[2])
    text_copy.start()
    pos_copy.start()
    image_copy.start()

    barrier = pltpu.get_barrier_semaphore()
    partners = [at_row(step) for step in range(1, RING)]
    partners += [((group + k) % 4, blk) for k in (1, 2, 3)]
    partners += [((group + k) % 4, other) for k in range(4)]
    for dev in partners:
        pl.semaphore_signal(barrier, inc=1, device_id=dev, device_id_type=MESH)
    pl.semaphore_wait(barrier, len(partners))

    def part_of(ref, slot, half, c):
        return ref.at[slot, pl.ds(c * CH, CH), pl.ds(half * H, H)]

    wrap_up = y // 3
    up_slot = 1 + 3 * wrap_up
    up_far = at_row(1 + 3 * wrap_up)
    far = at_row(3)

    def own_copy(stream, slot, half, c, dev):
        return rcopy(
            part_of(texts, 0, half, c), part_of(texts, slot, half, c),
            fetch_ss.at[stream, c], fetch_rs.at[slot, half, c], dev,
        )

    def arrived(slot, half, c):
        ref = part_of(texts, slot, half, c)
        rcopy(ref, ref, fetch_ss.at[0, c], fetch_rs.at[slot, half, c], up).wait_recv()

    def fwd_copy(stream, slot, half, c, dev):
        return rcopy(
            part_of(texts, slot, half, c), part_of(texts, 2, half, c),
            fwd_ss.at[stream, c], fetch_rs.at[2, half, c], dev,
        )

    def relay_copy(half, c):
        return rcopy(
            part_of(texts, 4, half, c), part_of(texts, 1, half, c),
            relay_ss.at[half, c], fetch_rs.at[1, half, c], at_row(-3),
        )

    text_copy.wait()
    for c in range(NC):
        own_copy(0, up_slot, 0, c, up_far).start()
        own_copy(1, 3, 1, c, far).start()
    image_copy.wait()
    own_image = images.at[pl.ds(2 * R, R)]
    to_other = rcopy(own_image, images.at[pl.ds(R, R)], img_ss.at[1], img_rs.at[1], handler_other)
    to_same = rcopy(own_image, images.at[pl.ds(0, R)], img_ss.at[0], img_rs.at[0], handler_same)
    to_other.start()
    to_same.start()

    def chunk_stats(ref, cols_ref, start, size):
        rows = pl.ds(start, size)
        lane = lax.broadcasted_iota(jnp.int32, (size, 128), 1)
        x = ref[rows, :]
        peak = jnp.max(x, axis=1, keepdims=True)
        total = jnp.sum(jnp.exp(x - peak), axis=1, keepdims=True)
        cols_ref[:, rows] = jnp.transpose(jnp.where(lane == 0, peak, total))[0:8, :]
        row_peak = jnp.max(x, axis=0, keepdims=True)
        return row_peak, jnp.sum(jnp.exp(x - row_peak), axis=0, keepdims=True)

    own_scores[...] = factor * dot_t(texts[0], images[pl.ds(2 * R, R), :])
    pos_copy.wait()
    positive = pos_vmem[...].reshape(1, R)
    mask = lax.broadcasted_iota(jnp.int32, (R, R), 0) == positive
    chosen = jnp.sum(jnp.where(mask, own_scores[...], 0.0))
    row_diag[...] = tile_of(*chunk_stats(own_scores, col_diag, 0, R))

    diag_same = rcopy(row_diag, row_owner.at[0], row_ss.at[3], row_rs.at[3], handler_same)
    diag_other = rcopy(row_diag, row_owner.at[1], row_ss.at[4], row_rs.at[4], handler_other)
    diag_same.start()
    diag_other.start()

    def forward(c, _):
        @pl.when(y == 3)
        def _():
            arrived(4, 0, c)
            relay_copy(0, c).start()

        arrived(1, 0, c)
        fwd_copy(0, 1, 0, c, up).start()
        arrived(3, 1, c)
        fwd_copy(1, 3, 1, c, down).start()
        own_copy(2, up_slot, 1, c, up_far).start()
        own_copy(3, 3, 0, c, far).start()
        return 0

    lax.fori_loop(0, NC, forward, 0)

    @pl.when(y == 3)
    def _():
        def relay(c, _):
            arrived(4, 1, c)
            relay_copy(1, c).start()
            return 0

        lax.fori_loop(0, NC, relay, 0)

    to_other.wait_recv()
    to_same.wait_recv()

    def keep_scores(d, start, x):
        rows = pl.ds(start, x.shape[0])
        scores[d, rows, :] = factor * x
        if d in (0, 3):
            @pl.when(xh == (1 if d == 0 else 0))
            def _():
                scores[d, rows, pl.ds(R, R)] = jnp.full((x.shape[0], R), LOW, F32)

        return chunk_stats(scores.at[d], col_part.at[d], start, x.shape[0])

    state = keep_scores(0, 0, dot_t(texts[0], images[pl.ds(0, 2 * R), :]))
    col_part[0] = tile_of(*merge([pair_of(col_part[0]), pair_of(col_diag[...])]))
    for c in range(NC):
        arrived(1, 1, c)
        arrived(3, 0, c)
        arrived(2, 0, c)
        arrived(2, 1, c)
        rows = pl.ds(c * CH, CH)
        joined = jnp.concatenate([texts[d, rows, :] for d in (1, 2, 3)], axis=0)
        x = dot_t(joined, images[pl.ds(0, 2 * R), :])
        state = merge([state] + [keep_scores(d, c * CH, x[(d - 1) * CH:d * CH, :]) for d in (1, 2, 3)])

    both = tile_of(*state)
    row_part[0] = both[:, 0:R]
    row_part[1] = both[:, R:2 * R]
    sends = []
    steps = (-1, 1, 2, -2, 3, -3)
    for k, step in enumerate(steps):
        low, high = max(0, -step), min(4, 4 - step)
        sends.append(rcopy(
            col_part.at[pl.ds(low, high - low)],
            col_peer.at[k, pl.ds(low + step, high - low)],
            col_ss.at[k], col_rs.at[k], at_row(step),
        ))
    sends.append(rcopy(row_part, row_peer, row_ss.at[0], row_rs.at[0], peer))
    sends.append(rcopy(row_part.at[0], row_back.at[0], row_ss.at[1], row_rs.at[1], owner_same))
    sends.append(rcopy(row_part.at[1], row_back.at[1], row_ss.at[2], row_rs.at[2], owner_other))
    from_peer, *from_handlers = sends[6:]
    for copy in [from_peer] + sends[:6] + from_handlers:
        copy.start()
    diag_same.wait_recv()
    diag_other.wait_recv()
    for copy in [from_peer] + sends[:3]:
        copy.wait_recv()

    def near_mate(k):
        place = (group * 2 + xh + k) % 8
        return (place // 2, big_y * 2 + place % 2)

    stages = [(group * 2 + xh, 8, near_mate), (big_y, RING, at_row)]

    def loss_copy(stage, k):
        place, _, mate = stages[stage]
        return rcopy(
            loss_out.at[stage], loss_in.at[stage, place],
            loss_ss.at[stage, k], loss_rs.at[stage, place], mate(k),
        )

    def loss_send(stage, value):
        place, count, _ = stages[stage]
        loss_out[stage] = value
        loss_in[stage, place] = value
        for k in range(1, count):
            loss_copy(stage, k).start()

    def loss_sum(stage):
        place, count, _ = stages[stage]
        for k in range(1, count):
            other_place = (place + k) % count
            rcopy(
                loss_out.at[stage], loss_in.at[stage, other_place],
                loss_ss.at[stage, k], loss_rs.at[stage, other_place], peer,
            ).wait_recv()
        return sum(loss_in[stage, i] for i in range(count))

    def lse(parts):
        peak, total = merge(parts)
        return peak + jnp.log(total)

    row_lse = jnp.concatenate(
        [lse([pair_of(row_part[k]), pair_of(row_peer[1 - k]), pair_of(row_owner[k])]) for k in range(2)],
        axis=1,
    )

    def col_lse(d):
        parts = [pair_of(col_part[d])]
        for k, step in enumerate(steps):
            if 0 <= d - step <= 3:
                parts.append(pair_of(col_peer[k, d]))
        value = lse(parts)
        col_column[d] = jnp.transpose(jnp.broadcast_to(value, (128, R)))
        return value

    def block_weights(d):
        for c in range(2):
            rows = pl.ds(c * (R // 2), R // 2)
            x = scores[d, rows, :]
            col = jnp.concatenate([col_column[d, rows, :]] * (2 * R // 128), axis=1)
            weights[d, rows, pl.ds(0, 2 * R)] = (jnp.exp(x - row_lse) + jnp.exp(x - col)).astype(BF16)

    def text_part(d, half):
        return dot_n(weights[d, :, pl.ds(0, 2 * R)], images[pl.ds(0, 2 * R), pl.ds(half * H, H)])

    def flip(d):
        weights_t[:, pl.ds(d * R, R)] = jnp.transpose(weights[d, :, pl.ds(0, 2 * R)])

    wrap_down = 1 - (y + 3) // 4
    down_slot = 2 * wrap_down
    down_far = at_row(-1 - 3 * wrap_down)
    back_far = at_row(-3)

    def cut(ref, half, c):
        return ref.at[pl.ds(c * CH, CH), pl.ds(half * H, H)]

    def half_copy(half, c, dev):
        return rcopy(
            cut(part2, half, c), half_in.at[half, pl.ds(c * CH, CH)],
            half_ss.at[half, c], half_rs.at[half, c], dev,
        )

    def part_copy(ref, stream, slot, half, c, dev):
        return rcopy(
            cut(ref, half, c), part_of(part_in, slot, half, c),
            part_ss.at[stream, half, c], part_rs.at[slot, half, c], dev,
        )

    def part_arrived(slot, half, c):
        ref = part_of(part_in, slot, half, c)
        rcopy(ref, ref, part_ss.at[0, half, c], part_rs.at[slot, half, c], up).wait_recv()

    def back_copy(half, c):
        return rcopy(
            part_of(part_in, 2, half, c), part_of(part_in, 0, half, c),
            back_ss.at[half, c], part_rs.at[0, half, c], at_row(3),
        )

    col_lse(2)
    block_weights(2)
    part2[:, pl.ds(0, H)] = text_part(2, 0).astype(BF16)
    for c in range(NC):
        half_copy(0, c, down).start()
    part2[:, pl.ds(H, H)] = text_part(2, 1).astype(BF16)
    for c in range(NC):
        half_copy(1, c, up).start()
    for copy in sends[3:6] + from_handlers:
        copy.wait_recv()
    own_row_lse = lse([pair_of(row_diag[...]), pair_of(row_back[0]), pair_of(row_back[1])])
    own_col_lse = col_lse(0)
    terms = jnp.sum(own_row_lse) + jnp.sum(own_col_lse) - 2.0 * chosen
    loss_send(0, jnp.full((8, 128), terms, F32))
    col_lse(1)
    block_weights(1)
    part1[:, pl.ds(H, H)] = text_part(1, 1).astype(BF16)
    for c in range(NC):
        part_copy(part1, 0, down_slot, 1, c, down_far).start()
    loss_send(1, loss_sum(0))
    col_lse(3)
    block_weights(3)
    part3[:, pl.ds(0, H)] = text_part(3, 0).astype(BF16)
    for c in range(NC):
        part_copy(part3, 1, 1, 0, c, back_far).start()
    stash1[...] = text_part(1, 0)
    stash3[...] = text_part(3, 1)

    def image_part(k):
        flat = texts.reshape(5 * R, D)[pl.ds(0, 4 * R), :]
        grad_send[k] = dot_n(weights_t[pl.ds(k * R, R), :], flat).astype(BF16)

    grad_other = rcopy(grad_send.at[1], grad_in.at[1], grad_ss.at[1], grad_rs.at[1], owner_other)
    grad_same = rcopy(grad_send.at[0], grad_in.at[0], grad_ss.at[0], grad_rs.at[0], owner_same)
    def add_halves(c):
        rows = pl.ds(c * CH, CH)
        half_copy(0, c, down).wait_recv()
        part1[rows, pl.ds(0, H)] = (stash1[rows, :] + half_in[0, rows, :].astype(F32)).astype(BF16)
        part_copy(part1, 0, down_slot, 0, c, down_far).start()
        half_copy(1, c, up).wait_recv()
        part3[rows, pl.ds(H, H)] = (stash3[rows, :] + half_in[1, rows, :].astype(F32)).astype(BF16)
        part_copy(part3, 1, 1, 1, c, back_far).start()

    def relay_parts(half):
        @pl.when(y == 0)
        def _():
            for c in range(NC):
                part_arrived(2, half, c)
                back_copy(half, c).start()

    add_halves(0)
    block_weights(0)
    for d in range(4):
        flip(d)
    image_part(1)
    grad_other.start()
    add_halves(1)
    image_part(0)
    grad_same.start()
    add_halves(2)
    relay_parts(1)

    x = own_scores[...]
    own_col = jnp.concatenate([col_column[0]] * (R // 128), axis=1)
    own_w = jnp.exp(x - own_row_lse) + jnp.exp(x - own_col)
    weights[0, :, pl.ds(2 * R, R)] = jnp.where(mask, own_w - 2.0, own_w).astype(BF16)
    own_weights_t[...] = jnp.transpose(weights[0, :, pl.ds(2 * R, R)])
    relay_parts(0)

    text_out[...] = dot_n(weights[0], images[...])
    image_out[...] = dot_n(own_weights_t[...], texts[0])


    grad_other.wait_recv()
    grad_same.wait_recv()

    def finish_image(c, _):
        rows = pl.ds(pl.multiple_of(c * CH, CH), CH)
        image_out[rows, :] = factor * (
            image_out[rows, :] + grad_in[0, rows, :].astype(F32) + grad_in[1, rows, :].astype(F32)
        )
        return 0

    lax.fori_loop(0, NC, finish_image, 0)

    def finish_text(c, _):
        rows = pl.ds(pl.multiple_of(c * CH, CH), CH)
        for slot in range(2):
            for half in range(2):
                part_arrived(slot, half, c)
        text_out[rows, :] = factor * (
            text_out[rows, :] + part_in[0, rows, :].astype(F32) + part_in[1, rows, :].astype(F32)
        )
        return 0

    lax.fori_loop(0, NC, finish_text, 0)

    to_other.wait_send()
    to_same.wait_send()
    for copy in sends + [diag_same, diag_other]:
        copy.wait_send()
    grad_other.wait_send()
    grad_same.wait_send()
    for stage, (_, count, _) in enumerate(stages):
        for k in range(1, count):
            loss_copy(stage, k).wait_send()
    loss_ref[0] = loss_sum(1)[0, 0] * (0.5 / (R * 128))

    def drain(c, _):
        own_copy(0, up_slot, 0, c, up_far).wait_send()
        own_copy(1, 3, 1, c, far).wait_send()
        own_copy(2, up_slot, 1, c, up_far).wait_send()
        own_copy(3, 3, 0, c, far).wait_send()
        fwd_copy(0, 1, 0, c, up).wait_send()
        fwd_copy(1, 3, 1, c, down).wait_send()
        half_copy(0, c, down).wait_send()
        half_copy(1, c, up).wait_send()
        for half in range(2):
            part_copy(part1, 0, down_slot, half, c, down_far).wait_send()
            part_copy(part3, 1, 1, half, c, back_far).wait_send()

        @pl.when(y == 3)
        def _():
            relay_copy(0, c).wait_send()
            relay_copy(1, c).wait_send()

        @pl.when(y == 0)
        def _():
            back_copy(0, c).wait_send()
            back_copy(1, c).wait_send()

        return 0

    lax.fori_loop(0, NC, drain, 0)


def on_device(image_emb, text_emb, positive, logit_scale):
    vmem, dma = pltpu.VMEM, pltpu.SemaphoreType.DMA
    return pl.pallas_call(
        kernel,
        out_shape=(
            jax.ShapeDtypeStruct((1,), F32),
            jax.ShapeDtypeStruct((R, D), F32),
            jax.ShapeDtypeStruct((R, D), F32),
        ),
        in_specs=[
            pl.BlockSpec(memory_space=pltpu.SMEM),
            pl.BlockSpec(memory_space=pltpu.HBM),
            pl.BlockSpec(memory_space=pltpu.HBM),
            pl.BlockSpec(memory_space=pltpu.HBM),
        ],
        out_specs=(
            pl.BlockSpec(memory_space=pltpu.SMEM),
            pl.BlockSpec(memory_space=pltpu.VMEM),
            pl.BlockSpec(memory_space=pltpu.VMEM),
        ),
        scratch_shapes=[
            vmem((5, R, D), BF16),
            vmem((3 * R, D), BF16),
            vmem((4, R, 2 * R), F32),
            vmem((R, R), F32),
            vmem((4, R, 3 * R), BF16),
            vmem((2 * R, 4 * R), BF16),
            vmem((R, R), BF16),
            vmem((4, R, 128), F32),
            vmem((2, 8, R), F32),
            vmem((8, R), F32),
            vmem((4, 8, R), F32),
            vmem((8, R), F32),
            vmem((2, 8, R), F32),
            vmem((2, 8, R), F32),
            vmem((2, 8, R), F32),
            vmem((6, 4, 8, R), F32),
            vmem((R, D), BF16),
            vmem((R, D), BF16),
            vmem((R, D), BF16),
            vmem((R, H), F32),
            vmem((R, H), F32),
            vmem((3, R, D), BF16),
            vmem((2, R, H), BF16),
            vmem((2, R, D), BF16),
            vmem((2, R, D), BF16),
            dma((3,)),
            dma((4, NC)),
            dma((5, 2, NC)),
            dma((2, NC)),
            dma((2, NC)),
            dma((2,)),
            dma((2,)),
            dma((5,)),
            dma((5,)),
            dma((6,)),
            dma((6,)),
            dma((2, NC)),
            dma((2, NC)),
            dma((2, 2, NC)),
            dma((3, 2, NC)),
            dma((2, NC)),
            dma((2,)),
            dma((2,)),
            vmem((2, 8, 128), F32),
            vmem((2, RING, 8, 128), F32),
            dma((2, RING)),
            dma((2, RING)),
            vmem((R,), jnp.int32),
        ],
        compiler_params=pltpu.CompilerParams(
            collective_id=0, has_side_effects=True, vmem_limit_bytes=42 * 1024 * 1024
        ),
    )(logit_scale, *(pltpu.with_memory_space_constraint(a, pltpu.HBM) for a in (image_emb, text_emb, positive)))


def solution(mesh):
    placed = (P(("group", "blk"), None), P(("group", "blk"), None), P(("group", "blk")), P())
    return jax.shard_map(
        on_device,
        mesh=mesh,
        in_specs=placed,
        out_specs=(P(), P(("group", "blk"), None), P(("group", "blk"), None)),
        check_vma=False,
    )
```

```python
import functools

import jax
import jax.numpy as jnp
from jax import lax
from jax.experimental import pallas as pl
from jax.experimental.pallas import tpu as pltpu
from jax.sharding import PartitionSpec as P

MESH = pl.DeviceIdType.MESH
F32 = jnp.float32
BF16 = jnp.bfloat16
R = 384
D = 1280
H = D // 2
NC = 6
CH = R // NC
SC = 128
PER = NC // 3
LOW = -1e30
RING = 16


def rcopy(src, dst, ss, rs, dev):
    return pltpu.make_async_remote_copy(
        src_ref=src, dst_ref=dst, send_sem=ss, recv_sem=rs, device_id=dev, device_id_type=MESH
    )


def dot_t(a, b):
    return lax.dot_general(a, b, (((1,), (1,)), ((), ())), preferred_element_type=F32)


def dot_n(a, b):
    return lax.dot_general(a, b, (((1,), (0,)), ((), ())), preferred_element_type=F32)


def merge(parts):
    peak = functools.reduce(jnp.maximum, [m for m, _ in parts])
    total = sum(s * jnp.exp(m - peak) for m, s in parts)
    return peak, total


def tile_of(peak, total):
    row = lax.broadcasted_iota(jnp.int32, (8, peak.shape[1]), 0)
    return jnp.where(row == 0, peak, total)


def pair_of(tile):
    return tile[0:1, :], tile[1:2, :]


def kernel(
    scale_ref, image_ref, text_ref, pos_ref,
    loss_ref, image_out, text_out,
    texts, images, scores, own_scores, weights, weights_t, own_weights_t,
    col_column, row_part, row_diag, col_part, col_diag,
    row_peer, row_owner, row_back, col_peer,
    part1, part2, part3, stash1, stash3, part_in, half_in,
    grad_send, grad_in,
    local_sem, fetch_ss, fetch_rs, fwd_ss, relay_ss, img_ss, img_rs,
    row_ss, row_rs, col_ss, col_rs,
    half_ss, half_rs, part_ss, part_rs, back_ss, grad_ss, grad_rs,
    loss_out, loss_in, loss_ss, loss_rs, pos_vmem,
):
    group = lax.axis_index("group")
    blk = lax.axis_index("blk")
    xh = blk % 2
    big_y = blk // 2
    y = big_y % 4
    factor = scale_ref[0]

    def at_row(step):
        return (group, ((big_y + step + RING) % RING) * 2 + xh)

    up, down = at_row(1), at_row(-1)
    behind = (group + 3) % 4
    ahead = (group + 1) % 4
    same, other = blk, big_y * 2 + (1 - xh)
    handler_same, handler_other = (behind, same), (behind, other)
    owner_same, owner_other = (ahead, same), (ahead, other)
    peer = (group, other)

    text_copy = pltpu.make_async_copy(text_ref, texts.at[0], local_sem.at[0])
    image_copy = pltpu.make_async_copy(image_ref, images.at[pl.ds(2 * R, R)], local_sem.at[1])
    pos_copy = pltpu.make_async_copy(pos_ref, pos_vmem, local_sem.at[2])
    text_copy.start()
    pos_copy.start()
    image_copy.start()

    barrier = pltpu.get_barrier_semaphore()
    partners = [at_row(step) for step in range(1, RING)]
    partners += [((group + k) % 4, blk) for k in (1, 2, 3)]
    partners += [((group + k) % 4, other) for k in range(4)]
    for dev in partners:
        pl.semaphore_signal(barrier, inc=1, device_id=dev, device_id_type=MESH)
    pl.semaphore_wait(barrier, len(partners))

    def part_of(ref, slot, half, c):
        return ref.at[slot, pl.ds(c * CH, CH), pl.ds(half * H, H)]

    wrap_up = y // 3
    up_slot = 1 + 3 * wrap_up
    up_far = at_row(1 + 3 * wrap_up)
    far = at_row(3)

    def own_copy(stream, slot, half, c, dev):
        return rcopy(
            part_of(texts, 0, half, c), part_of(texts, slot, half, c),
            fetch_ss.at[stream, c], fetch_rs.at[slot, half, c], dev,
        )

    def arrived(slot, half, c):
        ref = part_of(texts, slot, half, c)
        rcopy(ref, ref, fetch_ss.at[0, c], fetch_rs.at[slot, half, c], up).wait_recv()

    def fwd_copy(stream, slot, half, c, dev):
        return rcopy(
            part_of(texts, slot, half, c), part_of(texts, 2, half, c),
            fwd_ss.at[stream, c], fetch_rs.at[2, half, c], dev,
        )

    def relay_copy(half, c):
        return rcopy(
            part_of(texts, 4, half, c), part_of(texts, 1, half, c),
            relay_ss.at[half, c], fetch_rs.at[1, half, c], at_row(-3),
        )

    text_copy.wait()
    for c in range(NC):
        own_copy(0, up_slot, 0, c, up_far).start()
        own_copy(1, 3, 1, c, far).start()
    image_copy.wait()
    own_image = images.at[pl.ds(2 * R, R)]
    to_other = rcopy(own_image, images.at[pl.ds(R, R)], img_ss.at[1], img_rs.at[1], handler_other)
    to_same = rcopy(own_image, images.at[pl.ds(0, R)], img_ss.at[0], img_rs.at[0], handler_same)
    to_other.start()
    to_same.start()

    def chunk_stats(ref, cols_ref, start, size):
        rows = pl.ds(start, size)
        lane = lax.broadcasted_iota(jnp.int32, (size, 128), 1)
        x = ref[rows, :]
        peak = jnp.max(x, axis=1, keepdims=True)
        total = jnp.sum(jnp.exp(x - peak), axis=1, keepdims=True)
        cols_ref[:, rows] = jnp.transpose(jnp.where(lane == 0, peak, total))[0:8, :]
        row_peak = jnp.max(x, axis=0, keepdims=True)
        return row_peak, jnp.sum(jnp.exp(x - row_peak), axis=0, keepdims=True)

    own_scores[...] = factor * dot_t(texts[0], images[pl.ds(2 * R, R), :])
    pos_copy.wait()
    positive = pos_vmem[...].reshape(1, R)
    mask = lax.broadcasted_iota(jnp.int32, (R, R), 0) == positive
    chosen = jnp.sum(jnp.where(mask, own_scores[...], 0.0))
    row_diag[...] = tile_of(*chunk_stats(own_scores, col_diag, 0, R))

    diag_same = rcopy(row_diag, row_owner.at[0], row_ss.at[3], row_rs.at[3], handler_same)
    diag_other = rcopy(row_diag, row_owner.at[1], row_ss.at[4], row_rs.at[4], handler_other)
    diag_same.start()
    diag_other.start()

    def forward(c, _):
        @pl.when(y == 3)
        def _():
            arrived(4, 0, c)
            relay_copy(0, c).start()

        arrived(1, 0, c)
        fwd_copy(0, 1, 0, c, up).start()
        arrived(3, 1, c)
        fwd_copy(1, 3, 1, c, down).start()
        own_copy(2, up_slot, 1, c, up_far).start()
        own_copy(3, 3, 0, c, far).start()
        return 0

    lax.fori_loop(0, NC, forward, 0)

    @pl.when(y == 3)
    def _():
        def relay(c, _):
            arrived(4, 1, c)
            relay_copy(1, c).start()
            return 0

        lax.fori_loop(0, NC, relay, 0)

    to_other.wait_recv()
    to_same.wait_recv()

    def keep_scores(d, start, x):
        rows = pl.ds(start, x.shape[0])
        scores[d, rows, :] = factor * x
        if d in (0, 3):
            @pl.when(xh == (1 if d == 0 else 0))
            def _():
                scores[d, rows, pl.ds(R, R)] = jnp.full((x.shape[0], R), LOW, F32)

        return chunk_stats(scores.at[d], col_part.at[d], start, x.shape[0])

    state = keep_scores(0, 0, dot_t(texts[0], images[pl.ds(0, 2 * R), :]))
    col_part[0] = tile_of(*merge([pair_of(col_part[0]), pair_of(col_diag[...])]))
    for g in range(R // SC):
        for c in range(g * PER, (g + 1) * PER):
            arrived(1, 1, c)
            arrived(3, 0, c)
            arrived(2, 0, c)
            arrived(2, 1, c)
        rows = pl.ds(g * SC, SC)
        joined = jnp.concatenate([texts[d, rows, :] for d in (1, 2, 3)], axis=0)
        x = dot_t(joined, images[pl.ds(0, 2 * R), :])
        state = merge([state] + [keep_scores(d, g * SC, x[(d - 1) * SC:d * SC, :]) for d in (1, 2, 3)])

    both = tile_of(*state)
    row_part[0] = both[:, 0:R]
    row_part[1] = both[:, R:2 * R]
    sends = []
    steps = (-1, 1, 2, -2, 3, -3)
    for k, step in enumerate(steps):
        low, high = max(0, -step), min(4, 4 - step)
        sends.append(rcopy(
            col_part.at[pl.ds(low, high - low)],
            col_peer.at[k, pl.ds(low + step, high - low)],
            col_ss.at[k], col_rs.at[k], at_row(step),
        ))
    sends.append(rcopy(row_part, row_peer, row_ss.at[0], row_rs.at[0], peer))
    sends.append(rcopy(row_part.at[0], row_back.at[0], row_ss.at[1], row_rs.at[1], owner_same))
    sends.append(rcopy(row_part.at[1], row_back.at[1], row_ss.at[2], row_rs.at[2], owner_other))
    from_peer, *from_handlers = sends[6:]
    for copy in [from_peer] + sends[:6] + from_handlers:
        copy.start()
    diag_same.wait_recv()
    diag_other.wait_recv()
    for copy in [from_peer] + sends[:3]:
        copy.wait_recv()

    def near_mate(k):
        place = (group * 2 + xh + k) % 8
        return (place // 2, big_y * 2 + place % 2)

    stages = [(group * 2 + xh, 8, near_mate), (big_y, RING, at_row)]

    def loss_copy(stage, k):
        place, _, mate = stages[stage]
        return rcopy(
            loss_out.at[stage], loss_in.at[stage, place],
            loss_ss.at[stage, k], loss_rs.at[stage, place], mate(k),
        )

    def loss_send(stage, value):
        place, count, _ = stages[stage]
        loss_out[stage] = value
        loss_in[stage, place] = value
        for k in range(1, count):
            loss_copy(stage, k).start()

    def loss_sum(stage):
        place, count, _ = stages[stage]
        for k in range(1, count):
            other_place = (place + k) % count
            rcopy(
                loss_out.at[stage], loss_in.at[stage, other_place],
                loss_ss.at[stage, k], loss_rs.at[stage, other_place], peer,
            ).wait_recv()
        return sum(loss_in[stage, i] for i in range(count))

    def lse(parts):
        peak, total = merge(parts)
        return peak + jnp.log(total)

    row_lse = jnp.concatenate(
        [lse([pair_of(row_part[k]), pair_of(row_peer[1 - k]), pair_of(row_owner[k])]) for k in range(2)],
        axis=1,
    )

    def col_lse(d):
        parts = [pair_of(col_part[d])]
        for k, step in enumerate(steps):
            if 0 <= d - step <= 3:
                parts.append(pair_of(col_peer[k, d]))
        value = lse(parts)
        col_column[d] = jnp.transpose(jnp.broadcast_to(value, (128, R)))
        return value

    def block_weights(d):
        for c in range(2):
            rows = pl.ds(c * (R // 2), R // 2)
            x = scores[d, rows, :]
            col = jnp.concatenate([col_column[d, rows, :]] * (2 * R // 128), axis=1)
            weights[d, rows, pl.ds(0, 2 * R)] = (jnp.exp(x - row_lse) + jnp.exp(x - col)).astype(BF16)

    def text_part(d):
        return dot_n(weights[d, :, pl.ds(0, 2 * R)], images[pl.ds(0, 2 * R), :])

    def flip(d):
        weights_t[:, pl.ds(d * R, R)] = jnp.transpose(weights[d, :, pl.ds(0, 2 * R)])

    wrap_down = 1 - (y + 3) // 4
    down_slot = 2 * wrap_down
    down_far = at_row(-1 - 3 * wrap_down)
    back_far = at_row(-3)

    def cut(ref, half, c):
        return ref.at[pl.ds(c * CH, CH), pl.ds(half * H, H)]

    def half_copy(half, c, dev):
        return rcopy(
            cut(part2, half, c), half_in.at[half, pl.ds(c * CH, CH)],
            half_ss.at[half, c], half_rs.at[half, c], dev,
        )

    def part_copy(ref, stream, slot, half, c, dev):
        return rcopy(
            cut(ref, half, c), part_of(part_in, slot, half, c),
            part_ss.at[stream, half, c], part_rs.at[slot, half, c], dev,
        )

    def part_arrived(slot, half, c):
        ref = part_of(part_in, slot, half, c)
        rcopy(ref, ref, part_ss.at[0, half, c], part_rs.at[slot, half, c], up).wait_recv()

    def back_copy(half, c):
        return rcopy(
            part_of(part_in, 2, half, c), part_of(part_in, 0, half, c),
            back_ss.at[half, c], part_rs.at[0, half, c], at_row(3),
        )

    col_lse(2)
    block_weights(2)
    part2[...] = text_part(2).astype(BF16)
    for c in range(NC):
        half_copy(0, c, down).start()
        half_copy(1, c, up).start()
    for copy in sends[3:6] + from_handlers:
        copy.wait_recv()
    own_row_lse = lse([pair_of(row_diag[...]), pair_of(row_back[0]), pair_of(row_back[1])])
    own_col_lse = col_lse(0)
    terms = jnp.sum(own_row_lse) + jnp.sum(own_col_lse) - 2.0 * chosen
    loss_send(0, jnp.full((8, 128), terms, F32))
    col_lse(1)
    block_weights(1)
    whole = text_part(1)
    part1[:, pl.ds(H, H)] = whole[:, H:].astype(BF16)
    stash1[...] = whole[:, :H]
    for c in range(NC):
        part_copy(part1, 0, down_slot, 1, c, down_far).start()
    loss_send(1, loss_sum(0))
    col_lse(3)
    block_weights(3)
    whole = text_part(3)
    part3[:, pl.ds(0, H)] = whole[:, :H].astype(BF16)
    stash3[...] = whole[:, H:]
    for c in range(NC):
        part_copy(part3, 1, 1, 0, c, back_far).start()

    def image_part(k):
        flat = texts.reshape(5 * R, D)[pl.ds(0, 4 * R), :]
        grad_send[k] = dot_n(weights_t[pl.ds(k * R, R), :], flat).astype(BF16)

    grad_other = rcopy(grad_send.at[1], grad_in.at[1], grad_ss.at[1], grad_rs.at[1], owner_other)
    grad_same = rcopy(grad_send.at[0], grad_in.at[0], grad_ss.at[0], grad_rs.at[0], owner_same)
    def add_halves(c):
        rows = pl.ds(c * CH, CH)
        half_copy(0, c, down).wait_recv()
        part1[rows, pl.ds(0, H)] = (stash1[rows, :] + half_in[0, rows, :].astype(F32)).astype(BF16)
        part_copy(part1, 0, down_slot, 0, c, down_far).start()
        half_copy(1, c, up).wait_recv()
        part3[rows, pl.ds(H, H)] = (stash3[rows, :] + half_in[1, rows, :].astype(F32)).astype(BF16)
        part_copy(part3, 1, 1, 1, c, back_far).start()

    def relay_parts():
        @pl.when(y == 0)
        def _():
            for c in range(NC):
                for half in (1, 0):
                    part_arrived(2, half, c)
                    back_copy(half, c).start()

    for c in range(0 * PER, 1 * PER):
        add_halves(c)
    block_weights(0)
    for d in range(4):
        flip(d)
    image_part(1)
    grad_other.start()
    for c in range(1 * PER, 2 * PER):
        add_halves(c)
    image_part(0)
    grad_same.start()
    for c in range(2 * PER, 3 * PER):
        add_halves(c)

    x = own_scores[...]
    own_col = jnp.concatenate([col_column[0]] * (R // 128), axis=1)
    own_w = jnp.exp(x - own_row_lse) + jnp.exp(x - own_col)
    weights[0, :, pl.ds(2 * R, R)] = jnp.where(mask, own_w - 2.0, own_w).astype(BF16)
    own_weights_t[...] = jnp.transpose(weights[0, :, pl.ds(2 * R, R)])
    relay_parts()

    text_out[...] = dot_n(weights[0], images[...])
    image_out[...] = dot_n(own_weights_t[...], texts[0])


    grad_other.wait_recv()
    grad_same.wait_recv()

    def finish_image(c, _):
        rows = pl.ds(pl.multiple_of(c * CH, CH), CH)
        image_out[rows, :] = factor * (
            image_out[rows, :] + grad_in[0, rows, :].astype(F32) + grad_in[1, rows, :].astype(F32)
        )
        return 0

    lax.fori_loop(0, NC, finish_image, 0)

    def finish_text(c, _):
        rows = pl.ds(pl.multiple_of(c * CH, CH), CH)
        for slot in range(2):
            for half in range(2):
                part_arrived(slot, half, c)
        text_out[rows, :] = factor * (
            text_out[rows, :] + part_in[0, rows, :].astype(F32) + part_in[1, rows, :].astype(F32)
        )
        return 0

    lax.fori_loop(0, NC, finish_text, 0)

    to_other.wait_send()
    to_same.wait_send()
    for copy in sends + [diag_same, diag_other]:
        copy.wait_send()
    grad_other.wait_send()
    grad_same.wait_send()
    for stage, (_, count, _) in enumerate(stages):
        for k in range(1, count):
            loss_copy(stage, k).wait_send()
    loss_ref[0] = loss_sum(1)[0, 0] * (0.5 / (R * 128))

    def drain(c, _):
        own_copy(0, up_slot, 0, c, up_far).wait_send()
        own_copy(1, 3, 1, c, far).wait_send()
        own_copy(2, up_slot, 1, c, up_far).wait_send()
        own_copy(3, 3, 0, c, far).wait_send()
        fwd_copy(0, 1, 0, c, up).wait_send()
        fwd_copy(1, 3, 1, c, down).wait_send()
        half_copy(0, c, down).wait_send()
        half_copy(1, c, up).wait_send()
        for half in range(2):
            part_copy(part1, 0, down_slot, half, c, down_far).wait_send()
            part_copy(part3, 1, 1, half, c, back_far).wait_send()

        @pl.when(y == 3)
        def _():
            relay_copy(0, c).wait_send()
            relay_copy(1, c).wait_send()

        @pl.when(y == 0)
        def _():
            back_copy(0, c).wait_send()
            back_copy(1, c).wait_send()

        return 0

    lax.fori_loop(0, NC, drain, 0)


def on_device(image_emb, text_emb, positive, logit_scale):
    vmem, dma = pltpu.VMEM, pltpu.SemaphoreType.DMA
    return pl.pallas_call(
        kernel,
        out_shape=(
            jax.ShapeDtypeStruct((1,), F32),
            jax.ShapeDtypeStruct((R, D), F32),
            jax.ShapeDtypeStruct((R, D), F32),
        ),
        in_specs=[
            pl.BlockSpec(memory_space=pltpu.SMEM),
            pl.BlockSpec(memory_space=pltpu.HBM),
            pl.BlockSpec(memory_space=pltpu.HBM),
            pl.BlockSpec(memory_space=pltpu.HBM),
        ],
        out_specs=(
            pl.BlockSpec(memory_space=pltpu.SMEM),
            pl.BlockSpec(memory_space=pltpu.VMEM),
            pl.BlockSpec(memory_space=pltpu.VMEM),
        ),
        scratch_shapes=[
            vmem((5, R, D), BF16),
            vmem((3 * R, D), BF16),
            vmem((4, R, 2 * R), F32),
            vmem((R, R), F32),
            vmem((4, R, 3 * R), BF16),
            vmem((2 * R, 4 * R), BF16),
            vmem((R, R), BF16),
            vmem((4, R, 128), F32),
            vmem((2, 8, R), F32),
            vmem((8, R), F32),
            vmem((4, 8, R), F32),
            vmem((8, R), F32),
            vmem((2, 8, R), F32),
            vmem((2, 8, R), F32),
            vmem((2, 8, R), F32),
            vmem((6, 4, 8, R), F32),
            vmem((R, D), BF16),
            vmem((R, D), BF16),
            vmem((R, D), BF16),
            vmem((R, H), F32),
            vmem((R, H), F32),
            vmem((3, R, D), BF16),
            vmem((2, R, H), BF16),
            vmem((2, R, D), BF16),
            vmem((2, R, D), BF16),
            dma((3,)),
            dma((4, NC)),
            dma((5, 2, NC)),
            dma((2, NC)),
            dma((2, NC)),
            dma((2,)),
            dma((2,)),
            dma((5,)),
            dma((5,)),
            dma((6,)),
            dma((6,)),
            dma((2, NC)),
            dma((2, NC)),
            dma((2, 2, NC)),
            dma((3, 2, NC)),
            dma((2, NC)),
            dma((2,)),
            dma((2,)),
            vmem((2, 8, 128), F32),
            vmem((2, RING, 8, 128), F32),
            dma((2, RING)),
            dma((2, RING)),
            vmem((R,), jnp.int32),
        ],
        compiler_params=pltpu.CompilerParams(
            collective_id=0, has_side_effects=True, vmem_limit_bytes=42 * 1024 * 1024
        ),
    )(logit_scale, *(pltpu.with_memory_space_constraint(a, pltpu.HBM) for a in (image_emb, text_emb, positive)))


def solution(mesh):
    placed = (P(("group", "blk"), None), P(("group", "blk"), None), P(("group", "blk")), P())
    return jax.shard_map(
        on_device,
        mesh=mesh,
        in_specs=placed,
        out_specs=(P(), P(("group", "blk"), None), P(("group", "blk"), None)),
        check_vma=False,
    )
```

```python
import functools

import jax
import jax.numpy as jnp
from jax import lax
from jax.experimental import pallas as pl
from jax.experimental.pallas import tpu as pltpu
from jax.sharding import PartitionSpec as P

MESH = pl.DeviceIdType.MESH
F32 = jnp.float32
BF16 = jnp.bfloat16
R = 384
D = 1280
H = D // 2
NC = 6
CH = R // NC
SC = 128
PER = NC // 3
LOW = -1e30
RING = 16


def rcopy(src, dst, ss, rs, dev):
    return pltpu.make_async_remote_copy(
        src_ref=src, dst_ref=dst, send_sem=ss, recv_sem=rs, device_id=dev, device_id_type=MESH
    )


def dot_t(a, b):
    return lax.dot_general(a, b, (((1,), (1,)), ((), ())), preferred_element_type=F32)


def dot_n(a, b):
    return lax.dot_general(a, b, (((1,), (0,)), ((), ())), preferred_element_type=F32)


def merge(parts):
    peak = functools.reduce(jnp.maximum, [m for m, _ in parts])
    total = sum(s * jnp.exp(m - peak) for m, s in parts)
    return peak, total


def tile_of(peak, total):
    row = lax.broadcasted_iota(jnp.int32, (8, peak.shape[1]), 0)
    return jnp.where(row == 0, peak, total)


def pair_of(tile):
    return tile[0:1, :], tile[1:2, :]


def kernel(
    scale_ref, image_ref, text_ref, pos_ref,
    loss_ref, image_out, text_out,
    texts, images, scores, own_scores, weights, weights_t, own_weights_t,
    col_column, row_part, row_diag, col_part, col_diag,
    row_peer, row_owner, row_back, col_peer,
    part1, part2, part3, stash1, stash3, part_in, half_in,
    grad_send, grad_in,
    local_sem, fetch_ss, fetch_rs, fwd_ss, relay_ss, img_ss, img_rs,
    row_ss, row_rs, col_ss, col_rs,
    half_ss, half_rs, part_ss, part_rs, back_ss, grad_ss, grad_rs,
    loss_out, loss_in, loss_ss, loss_rs, pos_vmem,
):
    group = lax.axis_index("group")
    blk = lax.axis_index("blk")
    xh = blk % 2
    big_y = blk // 2
    y = big_y % 4
    factor = scale_ref[0]

    def at_row(step):
        return (group, ((big_y + step + RING) % RING) * 2 + xh)

    up, down = at_row(1), at_row(-1)
    behind = (group + 3) % 4
    ahead = (group + 1) % 4
    same, other = blk, big_y * 2 + (1 - xh)
    handler_same, handler_other = (behind, same), (behind, other)
    owner_same, owner_other = (ahead, same), (ahead, other)
    peer = (group, other)

    text_copy = pltpu.make_async_copy(text_ref, texts.at[0], local_sem.at[0])
    image_copy = pltpu.make_async_copy(image_ref, images.at[pl.ds(2 * R, R)], local_sem.at[1])
    pos_copy = pltpu.make_async_copy(pos_ref, pos_vmem, local_sem.at[2])
    text_copy.start()
    pos_copy.start()
    image_copy.start()

    barrier = pltpu.get_barrier_semaphore()
    partners = [at_row(step) for step in range(1, RING)]
    partners += [((group + k) % 4, blk) for k in (1, 2, 3)]
    partners += [((group + k) % 4, other) for k in range(4)]
    for dev in partners:
        pl.semaphore_signal(barrier, inc=1, device_id=dev, device_id_type=MESH)
    pl.semaphore_wait(barrier, len(partners))

    def part_of(ref, slot, half, c):
        return ref.at[slot, pl.ds(c * CH, CH), pl.ds(half * H, H)]

    wrap_up = y // 3
    up_slot = 1 + 3 * wrap_up
    up_far = at_row(1 + 3 * wrap_up)
    far = at_row(3)

    def own_copy(stream, slot, half, c, dev):
        return rcopy(
            part_of(texts, 0, half, c), part_of(texts, slot, half, c),
            fetch_ss.at[stream, c], fetch_rs.at[slot, half, c], dev,
        )

    def arrived(slot, half, c):
        ref = part_of(texts, slot, half, c)
        rcopy(ref, ref, fetch_ss.at[0, c], fetch_rs.at[slot, half, c], up).wait_recv()

    def fwd_copy(stream, slot, half, c, dev):
        return rcopy(
            part_of(texts, slot, half, c), part_of(texts, 2, half, c),
            fwd_ss.at[stream, c], fetch_rs.at[2, half, c], dev,
        )

    def relay_copy(half, c):
        return rcopy(
            part_of(texts, 4, half, c), part_of(texts, 1, half, c),
            relay_ss.at[half, c], fetch_rs.at[1, half, c], at_row(-3),
        )

    text_copy.wait()
    for c in range(NC):
        own_copy(0, up_slot, 0, c, up_far).start()
        own_copy(1, 3, 1, c, far).start()
    image_copy.wait()
    own_image = images.at[pl.ds(2 * R, R)]
    to_other = rcopy(own_image, images.at[pl.ds(R, R)], img_ss.at[1], img_rs.at[1], handler_other)
    to_same = rcopy(own_image, images.at[pl.ds(0, R)], img_ss.at[0], img_rs.at[0], handler_same)
    to_other.start()
    to_same.start()

    def chunk_stats(ref, cols_ref, start, size):
        rows = pl.ds(start, size)
        lane = lax.broadcasted_iota(jnp.int32, (size, 128), 1)
        x = ref[rows, :]
        peak = jnp.max(x, axis=1, keepdims=True)
        total = jnp.sum(jnp.exp(x - peak), axis=1, keepdims=True)
        cols_ref[:, rows] = jnp.transpose(jnp.where(lane == 0, peak, total))[0:8, :]
        row_peak = jnp.max(x, axis=0, keepdims=True)
        return row_peak, jnp.sum(jnp.exp(x - row_peak), axis=0, keepdims=True)

    own_scores[...] = factor * dot_t(texts[0], images[pl.ds(2 * R, R), :])
    pos_copy.wait()
    positive = pos_vmem[...].reshape(1, R)
    mask = lax.broadcasted_iota(jnp.int32, (R, R), 0) == positive
    chosen = jnp.sum(jnp.where(mask, own_scores[...], 0.0))
    row_diag[...] = tile_of(*chunk_stats(own_scores, col_diag, 0, R))

    diag_same = rcopy(row_diag, row_owner.at[0], row_ss.at[3], row_rs.at[3], handler_same)
    diag_other = rcopy(row_diag, row_owner.at[1], row_ss.at[4], row_rs.at[4], handler_other)
    diag_same.start()
    diag_other.start()

    def forward(c, _):
        @pl.when(y == 3)
        def _():
            arrived(4, 0, c)
            relay_copy(0, c).start()

        arrived(1, 0, c)
        fwd_copy(0, 1, 0, c, up).start()
        arrived(3, 1, c)
        fwd_copy(1, 3, 1, c, down).start()
        own_copy(2, up_slot, 1, c, up_far).start()
        own_copy(3, 3, 0, c, far).start()
        return 0

    lax.fori_loop(0, NC, forward, 0)

    @pl.when(y == 3)
    def _():
        def relay(c, _):
            arrived(4, 1, c)
            relay_copy(1, c).start()
            return 0

        lax.fori_loop(0, NC, relay, 0)

    to_other.wait_recv()
    to_same.wait_recv()

    def keep_scores(d, start, x):
        rows = pl.ds(start, x.shape[0])
        scores[d, rows, :] = factor * x
        if d in (0, 3):
            @pl.when(xh == (1 if d == 0 else 0))
            def _():
                scores[d, rows, pl.ds(R, R)] = jnp.full((x.shape[0], R), LOW, F32)

        return chunk_stats(scores.at[d], col_part.at[d], start, x.shape[0])

    state = keep_scores(0, 0, dot_t(texts[0], images[pl.ds(0, 2 * R), :]))
    col_part[0] = tile_of(*merge([pair_of(col_part[0]), pair_of(col_diag[...])]))
    for g in range(R // SC):
        for c in range(g * PER, (g + 1) * PER):
            arrived(1, 1, c)
            arrived(3, 0, c)
            arrived(2, 0, c)
            arrived(2, 1, c)
        rows = pl.ds(g * SC, SC)
        joined = jnp.concatenate([texts[d, rows, :] for d in (1, 2, 3)], axis=0)
        x = dot_t(joined, images[pl.ds(0, 2 * R), :])
        state = merge([state] + [keep_scores(d, g * SC, x[(d - 1) * SC:d * SC, :]) for d in (1, 2, 3)])

    both = tile_of(*state)
    row_part[0] = both[:, 0:R]
    row_part[1] = both[:, R:2 * R]
    sends = []
    steps = (-1, 1, 2, -2, 3, -3)
    for k, step in enumerate(steps):
        low, high = max(0, -step), min(4, 4 - step)
        sends.append(rcopy(
            col_part.at[pl.ds(low, high - low)],
            col_peer.at[k, pl.ds(low + step, high - low)],
            col_ss.at[k], col_rs.at[k], at_row(step),
        ))
    sends.append(rcopy(row_part, row_peer, row_ss.at[0], row_rs.at[0], peer))
    sends.append(rcopy(row_part.at[0], row_back.at[0], row_ss.at[1], row_rs.at[1], owner_same))
    sends.append(rcopy(row_part.at[1], row_back.at[1], row_ss.at[2], row_rs.at[2], owner_other))
    from_peer, *from_handlers = sends[6:]
    for copy in [from_peer] + sends[:6] + from_handlers:
        copy.start()
    diag_same.wait_recv()
    diag_other.wait_recv()
    for copy in [from_peer] + sends[:3]:
        copy.wait_recv()

    def near_mate(k):
        place = (group * 2 + xh + k) % 8
        return (place // 2, big_y * 2 + place % 2)

    stages = [(group * 2 + xh, 8, near_mate), (big_y, RING, at_row)]

    def loss_copy(stage, k):
        place, _, mate = stages[stage]
        return rcopy(
            loss_out.at[stage], loss_in.at[stage, place],
            loss_ss.at[stage, k], loss_rs.at[stage, place], mate(k),
        )

    def loss_send(stage, value):
        place, count, _ = stages[stage]
        loss_out[stage] = value
        loss_in[stage, place] = value
        for k in range(1, count):
            loss_copy(stage, k).start()

    def loss_sum(stage):
        place, count, _ = stages[stage]
        for k in range(1, count):
            other_place = (place + k) % count
            rcopy(
                loss_out.at[stage], loss_in.at[stage, other_place],
                loss_ss.at[stage, k], loss_rs.at[stage, other_place], peer,
            ).wait_recv()
        return sum(loss_in[stage, i] for i in range(count))

    def lse(parts):
        peak, total = merge(parts)
        return peak + jnp.log(total)

    row_lse = jnp.concatenate(
        [lse([pair_of(row_part[k]), pair_of(row_peer[1 - k]), pair_of(row_owner[k])]) for k in range(2)],
        axis=1,
    )

    def col_lse(d):
        parts = [pair_of(col_part[d])]
        for k, step in enumerate(steps):
            if 0 <= d - step <= 3:
                parts.append(pair_of(col_peer[k, d]))
        value = lse(parts)
        col_column[d] = jnp.transpose(jnp.broadcast_to(value, (128, R)))
        return value

    def block_weights(d):
        for c in range(2):
            rows = pl.ds(c * (R // 2), R // 2)
            x = scores[d, rows, :]
            col = jnp.concatenate([col_column[d, rows, :]] * (2 * R // 128), axis=1)
            weights[d, rows, pl.ds(0, 2 * R)] = (jnp.exp(x - row_lse) + jnp.exp(x - col)).astype(BF16)

    def text_part(d):
        return dot_n(weights[d, :, pl.ds(0, 2 * R)], images[pl.ds(0, 2 * R), :])

    def flip(d):
        weights_t[:, pl.ds(d * R, R)] = jnp.transpose(weights[d, :, pl.ds(0, 2 * R)])

    wrap_down = 1 - (y + 3) // 4
    down_slot = 2 * wrap_down
    down_far = at_row(-1 - 3 * wrap_down)
    back_far = at_row(-3)

    def cut(ref, half, c):
        return ref.at[pl.ds(c * CH, CH), pl.ds(half * H, H)]

    def half_copy(half, c, dev):
        return rcopy(
            cut(part2, half, c), half_in.at[half, pl.ds(c * CH, CH)],
            half_ss.at[half, c], half_rs.at[half, c], dev,
        )

    def part_copy(ref, stream, slot, half, c, dev):
        return rcopy(
            cut(ref, half, c), part_of(part_in, slot, half, c),
            part_ss.at[stream, half, c], part_rs.at[slot, half, c], dev,
        )

    def part_arrived(slot, half, c):
        ref = part_of(part_in, slot, half, c)
        rcopy(ref, ref, part_ss.at[0, half, c], part_rs.at[slot, half, c], up).wait_recv()

    def back_copy(half, c):
        return rcopy(
            part_of(part_in, 2, half, c), part_of(part_in, 0, half, c),
            back_ss.at[half, c], part_rs.at[0, half, c], at_row(3),
        )

    col_lse(2)
    block_weights(2)
    part2[...] = text_part(2).astype(BF16)
    for c in range(NC):
        half_copy(0, c, down).start()
        half_copy(1, c, up).start()
    for copy in sends[3:6] + from_handlers:
        copy.wait_recv()
    own_row_lse = lse([pair_of(row_diag[...]), pair_of(row_back[0]), pair_of(row_back[1])])
    own_col_lse = col_lse(0)
    terms = jnp.sum(own_row_lse) + jnp.sum(own_col_lse) - 2.0 * chosen
    loss_send(0, jnp.full((8, 128), terms, F32))
    col_lse(1)
    block_weights(1)
    whole = text_part(1)
    part1[:, pl.ds(H, H)] = whole[:, H:].astype(BF16)
    stash1[...] = whole[:, :H]
    for c in range(NC):
        part_copy(part1, 0, down_slot, 1, c, down_far).start()
    col_lse(3)
    block_weights(3)
    whole = text_part(3)
    part3[:, pl.ds(0, H)] = whole[:, :H].astype(BF16)
    stash3[...] = whole[:, H:]
    for c in range(NC):
        part_copy(part3, 1, 1, 0, c, back_far).start()

    def image_part(k):
        flat = texts.reshape(5 * R, D)[pl.ds(0, 4 * R), :]
        grad_send[k] = dot_n(weights_t[pl.ds(k * R, R), :], flat).astype(BF16)

    grad_other = rcopy(grad_send.at[1], grad_in.at[1], grad_ss.at[1], grad_rs.at[1], owner_other)
    grad_same = rcopy(grad_send.at[0], grad_in.at[0], grad_ss.at[0], grad_rs.at[0], owner_same)
    def add_halves(c):
        rows = pl.ds(c * CH, CH)
        half_copy(0, c, down).wait_recv()
        part1[rows, pl.ds(0, H)] = (stash1[rows, :] + half_in[0, rows, :].astype(F32)).astype(BF16)
        part_copy(part1, 0, down_slot, 0, c, down_far).start()
        half_copy(1, c, up).wait_recv()
        part3[rows, pl.ds(H, H)] = (stash3[rows, :] + half_in[1, rows, :].astype(F32)).astype(BF16)
        part_copy(part3, 1, 1, 1, c, back_far).start()

    def relay_parts():
        @pl.when(y == 0)
        def _():
            for c in range(NC):
                for half in (1, 0):
                    part_arrived(2, half, c)
                    back_copy(half, c).start()

    for c in range(0 * PER, 1 * PER):
        add_halves(c)
    block_weights(0)
    for d in range(4):
        flip(d)
    image_part(1)
    grad_other.start()
    loss_send(1, loss_sum(0))
    for c in range(1 * PER, 2 * PER):
        add_halves(c)
    image_part(0)
    grad_same.start()
    for c in range(2 * PER, 3 * PER):
        add_halves(c)

    x = own_scores[...]
    own_col = jnp.concatenate([col_column[0]] * (R // 128), axis=1)
    own_w = jnp.exp(x - own_row_lse) + jnp.exp(x - own_col)
    weights[0, :, pl.ds(2 * R, R)] = jnp.where(mask, own_w - 2.0, own_w).astype(BF16)
    own_weights_t[...] = jnp.transpose(weights[0, :, pl.ds(2 * R, R)])
    relay_parts()

    text_out[...] = dot_n(weights[0], images[...])
    image_out[...] = dot_n(own_weights_t[...], texts[0])


    grad_other.wait_recv()
    grad_same.wait_recv()

    def finish_image(c, _):
        rows = pl.ds(pl.multiple_of(c * CH, CH), CH)
        image_out[rows, :] = factor * (
            image_out[rows, :] + grad_in[0, rows, :].astype(F32) + grad_in[1, rows, :].astype(F32)
        )
        return 0

    lax.fori_loop(0, NC, finish_image, 0)

    def finish_text(c, _):
        rows = pl.ds(pl.multiple_of(c * CH, CH), CH)
        for slot in range(2):
            for half in range(2):
                part_arrived(slot, half, c)
        text_out[rows, :] = factor * (
            text_out[rows, :] + part_in[0, rows, :].astype(F32) + part_in[1, rows, :].astype(F32)
        )
        return 0

    lax.fori_loop(0, NC, finish_text, 0)

    to_other.wait_send()
    to_same.wait_send()
    for copy in sends + [diag_same, diag_other]:
        copy.wait_send()
    grad_other.wait_send()
    grad_same.wait_send()
    for stage, (_, count, _) in enumerate(stages):
        for k in range(1, count):
            loss_copy(stage, k).wait_send()
    loss_ref[0] = loss_sum(1)[0, 0] * (0.5 / (R * 128))

    def drain(c, _):
        own_copy(0, up_slot, 0, c, up_far).wait_send()
        own_copy(1, 3, 1, c, far).wait_send()
        own_copy(2, up_slot, 1, c, up_far).wait_send()
        own_copy(3, 3, 0, c, far).wait_send()
        fwd_copy(0, 1, 0, c, up).wait_send()
        fwd_copy(1, 3, 1, c, down).wait_send()
        half_copy(0, c, down).wait_send()
        half_copy(1, c, up).wait_send()
        for half in range(2):
            part_copy(part1, 0, down_slot, half, c, down_far).wait_send()
            part_copy(part3, 1, 1, half, c, back_far).wait_send()

        @pl.when(y == 3)
        def _():
            relay_copy(0, c).wait_send()
            relay_copy(1, c).wait_send()

        @pl.when(y == 0)
        def _():
            back_copy(0, c).wait_send()
            back_copy(1, c).wait_send()

        return 0

    lax.fori_loop(0, NC, drain, 0)


def on_device(image_emb, text_emb, positive, logit_scale):
    vmem, dma = pltpu.VMEM, pltpu.SemaphoreType.DMA
    return pl.pallas_call(
        kernel,
        out_shape=(
            jax.ShapeDtypeStruct((1,), F32),
            jax.ShapeDtypeStruct((R, D), F32),
            jax.ShapeDtypeStruct((R, D), F32),
        ),
        in_specs=[
            pl.BlockSpec(memory_space=pltpu.SMEM),
            pl.BlockSpec(memory_space=pltpu.HBM),
            pl.BlockSpec(memory_space=pltpu.HBM),
            pl.BlockSpec(memory_space=pltpu.HBM),
        ],
        out_specs=(
            pl.BlockSpec(memory_space=pltpu.SMEM),
            pl.BlockSpec(memory_space=pltpu.VMEM),
            pl.BlockSpec(memory_space=pltpu.VMEM),
        ),
        scratch_shapes=[
            vmem((5, R, D), BF16),
            vmem((3 * R, D), BF16),
            vmem((4, R, 2 * R), F32),
            vmem((R, R), F32),
            vmem((4, R, 3 * R), BF16),
            vmem((2 * R, 4 * R), BF16),
            vmem((R, R), BF16),
            vmem((4, R, 128), F32),
            vmem((2, 8, R), F32),
            vmem((8, R), F32),
            vmem((4, 8, R), F32),
            vmem((8, R), F32),
            vmem((2, 8, R), F32),
            vmem((2, 8, R), F32),
            vmem((2, 8, R), F32),
            vmem((6, 4, 8, R), F32),
            vmem((R, D), BF16),
            vmem((R, D), BF16),
            vmem((R, D), BF16),
            vmem((R, H), F32),
            vmem((R, H), F32),
            vmem((3, R, D), BF16),
            vmem((2, R, H), BF16),
            vmem((2, R, D), BF16),
            vmem((2, R, D), BF16),
            dma((3,)),
            dma((4, NC)),
            dma((5, 2, NC)),
            dma((2, NC)),
            dma((2, NC)),
            dma((2,)),
            dma((2,)),
            dma((5,)),
            dma((5,)),
            dma((6,)),
            dma((6,)),
            dma((2, NC)),
            dma((2, NC)),
            dma((2, 2, NC)),
            dma((3, 2, NC)),
            dma((2, NC)),
            dma((2,)),
            dma((2,)),
            vmem((2, 8, 128), F32),
            vmem((2, RING, 8, 128), F32),
            dma((2, RING)),
            dma((2, RING)),
            vmem((R,), jnp.int32),
        ],
        compiler_params=pltpu.CompilerParams(
            collective_id=0, has_side_effects=True, vmem_limit_bytes=42 * 1024 * 1024
        ),
    )(logit_scale, *(pltpu.with_memory_space_constraint(a, pltpu.HBM) for a in (image_emb, text_emb, positive)))


def solution(mesh):
    placed = (P(("group", "blk"), None), P(("group", "blk"), None), P(("group", "blk")), P())
    return jax.shard_map(
        on_device,
        mesh=mesh,
        in_specs=placed,
        out_specs=(P(), P(("group", "blk"), None), P(("group", "blk"), None)),
        check_vma=False,
    )
```

```python
import functools

import jax
import jax.numpy as jnp
from jax import lax
from jax.experimental import pallas as pl
from jax.experimental.pallas import tpu as pltpu
from jax.sharding import PartitionSpec as P

MESH = pl.DeviceIdType.MESH
F32 = jnp.float32
BF16 = jnp.bfloat16
R = 384
D = 1280
H = D // 2
NC = 6
CH = R // NC
SC = 128
PER = NC // 3
LOW = -1e30
RING = 16


def rcopy(src, dst, ss, rs, dev):
    return pltpu.make_async_remote_copy(
        src_ref=src, dst_ref=dst, send_sem=ss, recv_sem=rs, device_id=dev, device_id_type=MESH
    )


def dot_t(a, b):
    return lax.dot_general(a, b, (((1,), (1,)), ((), ())), preferred_element_type=F32)


def dot_n(a, b):
    return lax.dot_general(a, b, (((1,), (0,)), ((), ())), preferred_element_type=F32)


def merge(parts):
    peak = functools.reduce(jnp.maximum, [m for m, _ in parts])
    total = sum(s * jnp.exp(m - peak) for m, s in parts)
    return peak, total


def tile_of(peak, total):
    row = lax.broadcasted_iota(jnp.int32, (8, peak.shape[1]), 0)
    return jnp.where(row == 0, peak, total)


def pair_of(tile):
    return tile[0:1, :], tile[1:2, :]


def kernel(
    scale_ref, image_ref, text_ref, pos_ref,
    loss_ref, image_out, text_out,
    texts, images, scores, own_scores, weights, weights_t, own_weights_t,
    col_column, row_part, row_diag, col_part, col_diag,
    row_peer, row_owner, row_back, col_peer,
    part1, part2, part3, stash1, stash3, part_in, half_in,
    grad_send, grad_in,
    local_sem, fetch_ss, fetch_rs, fwd_ss, relay_ss, img_ss, img_rs,
    row_ss, row_rs, col_ss, col_rs,
    half_ss, half_rs, part_ss, part_rs, back_ss, grad_ss, grad_rs,
    loss_out, loss_in, loss_ss, loss_rs, pos_vmem,
):
    group = lax.axis_index("group")
    blk = lax.axis_index("blk")
    xh = blk % 2
    big_y = blk // 2
    y = big_y % 4
    factor = scale_ref[0]

    def at_row(step):
        return (group, ((big_y + step + RING) % RING) * 2 + xh)

    up, down = at_row(1), at_row(-1)
    behind = (group + 3) % 4
    ahead = (group + 1) % 4
    same, other = blk, big_y * 2 + (1 - xh)
    handler_same, handler_other = (behind, same), (behind, other)
    owner_same, owner_other = (ahead, same), (ahead, other)
    peer = (group, other)

    text_copy = pltpu.make_async_copy(text_ref, texts.at[0], local_sem.at[0])
    image_copy = pltpu.make_async_copy(image_ref, images.at[pl.ds(2 * R, R)], local_sem.at[1])
    pos_copy = pltpu.make_async_copy(pos_ref, pos_vmem, local_sem.at[2])
    text_copy.start()
    pos_copy.start()
    image_copy.start()

    barrier = pltpu.get_barrier_semaphore()
    partners = [at_row(step) for step in range(1, RING)]
    partners += [((group + k) % 4, blk) for k in (1, 2, 3)]
    partners += [((group + k) % 4, other) for k in range(4)]
    for dev in partners:
        pl.semaphore_signal(barrier, inc=1, device_id=dev, device_id_type=MESH)
    pl.semaphore_wait(barrier, len(partners))

    def part_of(ref, slot, half, c):
        return ref.at[slot, pl.ds(c * CH, CH), pl.ds(half * H, H)]

    wrap_up = y // 3
    up_slot = 1 + 3 * wrap_up
    up_far = at_row(1 + 3 * wrap_up)
    far = at_row(3)

    def own_copy(stream, slot, half, c, dev):
        return rcopy(
            part_of(texts, 0, half, c), part_of(texts, slot, half, c),
            fetch_ss.at[stream, c], fetch_rs.at[slot, half, c], dev,
        )

    def arrived(slot, half, c):
        ref = part_of(texts, slot, half, c)
        rcopy(ref, ref, fetch_ss.at[0, c], fetch_rs.at[slot, half, c], up).wait_recv()

    def fwd_copy(stream, slot, half, c, dev):
        return rcopy(
            part_of(texts, slot, half, c), part_of(texts, 2, half, c),
            fwd_ss.at[stream, c], fetch_rs.at[2, half, c], dev,
        )

    def relay_copy(half, c):
        return rcopy(
            part_of(texts, 4, half, c), part_of(texts, 1, half, c),
            relay_ss.at[half, c], fetch_rs.at[1, half, c], at_row(-3),
        )

    text_copy.wait()
    for c in range(NC):
        own_copy(0, up_slot, 0, c, up_far).start()
        own_copy(1, 3, 1, c, far).start()
    image_copy.wait()
    own_image = images.at[pl.ds(2 * R, R)]
    to_other = rcopy(own_image, images.at[pl.ds(R, R)], img_ss.at[1], img_rs.at[1], handler_other)
    to_same = rcopy(own_image, images.at[pl.ds(0, R)], img_ss.at[0], img_rs.at[0], handler_same)
    to_other.start()
    to_same.start()

    def chunk_stats(ref, cols_ref, start, size):
        rows = pl.ds(start, size)
        lane = lax.broadcasted_iota(jnp.int32, (size, 128), 1)
        x = ref[rows, :]
        peak = jnp.max(x, axis=1, keepdims=True)
        total = jnp.sum(jnp.exp(x - peak), axis=1, keepdims=True)
        cols_ref[:, rows] = jnp.transpose(jnp.where(lane == 0, peak, total))[0:8, :]
        row_peak = jnp.max(x, axis=0, keepdims=True)
        return row_peak, jnp.sum(jnp.exp(x - row_peak), axis=0, keepdims=True)

    own_scores[...] = factor * dot_t(texts[0], images[pl.ds(2 * R, R), :])
    pos_copy.wait()
    positive = pos_vmem[...].reshape(1, R)
    mask = lax.broadcasted_iota(jnp.int32, (R, R), 0) == positive
    chosen = jnp.sum(jnp.where(mask, own_scores[...], 0.0))
    row_diag[...] = tile_of(*chunk_stats(own_scores, col_diag, 0, R))

    diag_same = rcopy(row_diag, row_owner.at[0], row_ss.at[3], row_rs.at[3], handler_same)
    diag_other = rcopy(row_diag, row_owner.at[1], row_ss.at[4], row_rs.at[4], handler_other)
    diag_same.start()
    diag_other.start()

    def forward(c, _):
        @pl.when(y == 3)
        def _():
            arrived(4, 0, c)
            relay_copy(0, c).start()

        arrived(1, 0, c)
        fwd_copy(0, 1, 0, c, up).start()
        arrived(3, 1, c)
        fwd_copy(1, 3, 1, c, down).start()
        own_copy(2, up_slot, 1, c, up_far).start()
        own_copy(3, 3, 0, c, far).start()
        return 0

    lax.fori_loop(0, NC, forward, 0)

    @pl.when(y == 3)
    def _():
        def relay(c, _):
            arrived(4, 1, c)
            relay_copy(1, c).start()
            return 0

        lax.fori_loop(0, NC, relay, 0)

    to_other.wait_recv()
    to_same.wait_recv()

    def keep_scores(d, start, x):
        rows = pl.ds(start, x.shape[0])
        scores[d, rows, :] = factor * x
        if d in (0, 3):
            @pl.when(xh == (1 if d == 0 else 0))
            def _():
                scores[d, rows, pl.ds(R, R)] = jnp.full((x.shape[0], R), LOW, F32)

        return chunk_stats(scores.at[d], col_part.at[d], start, x.shape[0])

    state = keep_scores(0, 0, dot_t(texts[0], images[pl.ds(0, 2 * R), :]))
    col_part[0] = tile_of(*merge([pair_of(col_part[0]), pair_of(col_diag[...])]))
    for g in range(R // SC):
        for c in range(g * PER, (g + 1) * PER):
            arrived(1, 1, c)
            arrived(3, 0, c)
            arrived(2, 0, c)
            arrived(2, 1, c)
        rows = pl.ds(g * SC, SC)
        joined = jnp.concatenate([texts[d, rows, :] for d in (1, 2, 3)], axis=0)
        x = dot_t(joined, images[pl.ds(0, 2 * R), :])
        state = merge([state] + [keep_scores(d, g * SC, x[(d - 1) * SC:d * SC, :]) for d in (1, 2, 3)])

    both = tile_of(*state)
    row_part[0] = both[:, 0:R]
    row_part[1] = both[:, R:2 * R]
    sends = []
    steps = (-1, 1, 2, -2, 3, -3)
    for k, step in enumerate(steps):
        low, high = max(0, -step), min(4, 4 - step)
        sends.append(rcopy(
            col_part.at[pl.ds(low, high - low)],
            col_peer.at[k, pl.ds(low + step, high - low)],
            col_ss.at[k], col_rs.at[k], at_row(step),
        ))
    sends.append(rcopy(row_part, row_peer, row_ss.at[0], row_rs.at[0], peer))
    sends.append(rcopy(row_part.at[0], row_back.at[0], row_ss.at[1], row_rs.at[1], owner_same))
    sends.append(rcopy(row_part.at[1], row_back.at[1], row_ss.at[2], row_rs.at[2], owner_other))
    from_peer, *from_handlers = sends[6:]
    for copy in [from_peer] + sends[:6] + from_handlers:
        copy.start()
    diag_same.wait_recv()
    diag_other.wait_recv()
    for copy in [from_peer] + sends[:3]:
        copy.wait_recv()

    def near_mate(k):
        place = (group * 2 + xh + k) % 8
        return (place // 2, big_y * 2 + place % 2)

    stages = [(group * 2 + xh, 8, near_mate), (big_y, RING, at_row)]

    def loss_copy(stage, k):
        place, _, mate = stages[stage]
        return rcopy(
            loss_out.at[stage], loss_in.at[stage, place],
            loss_ss.at[stage, k], loss_rs.at[stage, place], mate(k),
        )

    def loss_send(stage, value):
        place, count, _ = stages[stage]
        loss_out[stage] = value
        loss_in[stage, place] = value
        for k in range(1, count):
            loss_copy(stage, k).start()

    def loss_sum(stage):
        place, count, _ = stages[stage]
        for k in range(1, count):
            other_place = (place + k) % count
            rcopy(
                loss_out.at[stage], loss_in.at[stage, other_place],
                loss_ss.at[stage, k], loss_rs.at[stage, other_place], peer,
            ).wait_recv()
        return sum(loss_in[stage, i] for i in range(count))

    def lse(parts):
        peak, total = merge(parts)
        return peak + jnp.log(total)

    row_lse = jnp.concatenate(
        [lse([pair_of(row_part[k]), pair_of(row_peer[1 - k]), pair_of(row_owner[k])]) for k in range(2)],
        axis=1,
    )

    def col_lse(d):
        parts = [pair_of(col_part[d])]
        for k, step in enumerate(steps):
            if 0 <= d - step <= 3:
                parts.append(pair_of(col_peer[k, d]))
        value = lse(parts)
        col_column[d] = jnp.transpose(jnp.broadcast_to(value, (128, R)))
        return value

    def block_weights(d):
        for c in range(2):
            rows = pl.ds(c * (R // 2), R // 2)
            x = scores[d, rows, :]
            col = jnp.concatenate([col_column[d, rows, :]] * (2 * R // 128), axis=1)
            weights[d, rows, pl.ds(0, 2 * R)] = (jnp.exp(x - row_lse) + jnp.exp(x - col)).astype(BF16)

    def text_part(d):
        return dot_n(weights[d, :, pl.ds(0, 2 * R)], images[pl.ds(0, 2 * R), :])

    def flip(d):
        weights_t[:, pl.ds(d * R, R)] = jnp.transpose(weights[d, :, pl.ds(0, 2 * R)])

    wrap_down = 1 - (y + 3) // 4
    down_slot = 2 * wrap_down
    down_far = at_row(-1 - 3 * wrap_down)
    back_far = at_row(-3)

    def cut(ref, half, c):
        return ref.at[pl.ds(c * CH, CH), pl.ds(half * H, H)]

    def half_copy(half, c, dev):
        return rcopy(
            cut(part2, half, c), half_in.at[half, pl.ds(c * CH, CH)],
            half_ss.at[half, c], half_rs.at[half, c], dev,
        )

    def part_copy(ref, stream, slot, half, c, dev):
        return rcopy(
            cut(ref, half, c), part_of(part_in, slot, half, c),
            part_ss.at[stream, half, c], part_rs.at[slot, half, c], dev,
        )

    def part_arrived(slot, half, c):
        ref = part_of(part_in, slot, half, c)
        rcopy(ref, ref, part_ss.at[0, half, c], part_rs.at[slot, half, c], up).wait_recv()

    def back_copy(half, c):
        return rcopy(
            part_of(part_in, 2, half, c), part_of(part_in, 0, half, c),
            back_ss.at[half, c], part_rs.at[0, half, c], at_row(3),
        )

    col_lse(2)
    block_weights(2)
    part2[...] = text_part(2).astype(BF16)
    for c in range(NC):
        half_copy(0, c, down).start()
        half_copy(1, c, up).start()
    for copy in sends[3:6] + from_handlers:
        copy.wait_recv()
    own_row_lse = lse([pair_of(row_diag[...]), pair_of(row_back[0]), pair_of(row_back[1])])
    own_col_lse = col_lse(0)
    terms = jnp.sum(own_row_lse) + jnp.sum(own_col_lse) - 2.0 * chosen
    loss_send(0, jnp.full((8, 128), terms, F32))
    col_lse(1)
    block_weights(1)
    whole = text_part(1)
    part1[:, pl.ds(H, H)] = whole[:, H:].astype(BF16)
    stash1[...] = whole[:, :H]
    for c in range(NC):
        part_copy(part1, 0, down_slot, 1, c, down_far).start()
    col_lse(3)
    block_weights(3)
    whole = text_part(3)
    part3[:, pl.ds(0, H)] = whole[:, :H].astype(BF16)
    stash3[...] = whole[:, H:]
    for c in range(NC):
        part_copy(part3, 1, 1, 0, c, back_far).start()

    def image_part(k):
        flat = texts.reshape(5 * R, D)[pl.ds(0, 4 * R), :]
        grad_send[k] = dot_n(weights_t[pl.ds(k * R, R), :], flat).astype(BF16)

    grad_other = rcopy(grad_send.at[1], grad_in.at[1], grad_ss.at[1], grad_rs.at[1], owner_other)
    grad_same = rcopy(grad_send.at[0], grad_in.at[0], grad_ss.at[0], grad_rs.at[0], owner_same)
    def add_halves(c):
        rows = pl.ds(c * CH, CH)
        half_copy(0, c, down).wait_recv()
        part1[rows, pl.ds(0, H)] = (stash1[rows, :] + half_in[0, rows, :].astype(F32)).astype(BF16)
        part_copy(part1, 0, down_slot, 0, c, down_far).start()
        half_copy(1, c, up).wait_recv()
        part3[rows, pl.ds(H, H)] = (stash3[rows, :] + half_in[1, rows, :].astype(F32)).astype(BF16)
        part_copy(part3, 1, 1, 1, c, back_far).start()

    def relay_parts():
        @pl.when(y == 0)
        def _():
            for c in range(NC):
                for half in (1, 0):
                    part_arrived(2, half, c)
                    back_copy(half, c).start()

    block_weights(0)
    for d in range(4):
        flip(d)
    image_part(1)
    grad_other.start()
    loss_send(1, loss_sum(0))
    for c in range(0, 2 * PER):
        add_halves(c)
    image_part(0)
    grad_same.start()
    for c in range(2 * PER, 3 * PER):
        add_halves(c)

    x = own_scores[...]
    own_col = jnp.concatenate([col_column[0]] * (R // 128), axis=1)
    own_w = jnp.exp(x - own_row_lse) + jnp.exp(x - own_col)
    weights[0, :, pl.ds(2 * R, R)] = jnp.where(mask, own_w - 2.0, own_w).astype(BF16)
    own_weights_t[...] = jnp.transpose(weights[0, :, pl.ds(2 * R, R)])
    relay_parts()

    text_out[...] = dot_n(weights[0], images[...])
    image_out[...] = dot_n(own_weights_t[...], texts[0])


    grad_other.wait_recv()
    grad_same.wait_recv()

    def finish_image(c, _):
        rows = pl.ds(pl.multiple_of(c * CH, CH), CH)
        image_out[rows, :] = factor * (
            image_out[rows, :] + grad_in[0, rows, :].astype(F32) + grad_in[1, rows, :].astype(F32)
        )
        return 0

    lax.fori_loop(0, NC, finish_image, 0)

    def finish_text(c, _):
        rows = pl.ds(pl.multiple_of(c * CH, CH), CH)
        for slot in range(2):
            for half in range(2):
                part_arrived(slot, half, c)
        text_out[rows, :] = factor * (
            text_out[rows, :] + part_in[0, rows, :].astype(F32) + part_in[1, rows, :].astype(F32)
        )
        return 0

    lax.fori_loop(0, NC, finish_text, 0)

    to_other.wait_send()
    to_same.wait_send()
    for copy in sends + [diag_same, diag_other]:
        copy.wait_send()
    grad_other.wait_send()
    grad_same.wait_send()
    for stage, (_, count, _) in enumerate(stages):
        for k in range(1, count):
            loss_copy(stage, k).wait_send()
    loss_ref[0] = loss_sum(1)[0, 0] * (0.5 / (R * 128))

    def drain(c, _):
        own_copy(0, up_slot, 0, c, up_far).wait_send()
        own_copy(1, 3, 1, c, far).wait_send()
        own_copy(2, up_slot, 1, c, up_far).wait_send()
        own_copy(3, 3, 0, c, far).wait_send()
        fwd_copy(0, 1, 0, c, up).wait_send()
        fwd_copy(1, 3, 1, c, down).wait_send()
        half_copy(0, c, down).wait_send()
        half_copy(1, c, up).wait_send()
        for half in range(2):
            part_copy(part1, 0, down_slot, half, c, down_far).wait_send()
            part_copy(part3, 1, 1, half, c, back_far).wait_send()

        @pl.when(y == 3)
        def _():
            relay_copy(0, c).wait_send()
            relay_copy(1, c).wait_send()

        @pl.when(y == 0)
        def _():
            back_copy(0, c).wait_send()
            back_copy(1, c).wait_send()

        return 0

    lax.fori_loop(0, NC, drain, 0)


def on_device(image_emb, text_emb, positive, logit_scale):
    vmem, dma = pltpu.VMEM, pltpu.SemaphoreType.DMA
    return pl.pallas_call(
        kernel,
        out_shape=(
            jax.ShapeDtypeStruct((1,), F32),
            jax.ShapeDtypeStruct((R, D), F32),
            jax.ShapeDtypeStruct((R, D), F32),
        ),
        in_specs=[
            pl.BlockSpec(memory_space=pltpu.SMEM),
            pl.BlockSpec(memory_space=pltpu.HBM),
            pl.BlockSpec(memory_space=pltpu.HBM),
            pl.BlockSpec(memory_space=pltpu.HBM),
        ],
        out_specs=(
            pl.BlockSpec(memory_space=pltpu.SMEM),
            pl.BlockSpec(memory_space=pltpu.VMEM),
            pl.BlockSpec(memory_space=pltpu.VMEM),
        ),
        scratch_shapes=[
            vmem((5, R, D), BF16),
            vmem((3 * R, D), BF16),
            vmem((4, R, 2 * R), F32),
            vmem((R, R), F32),
            vmem((4, R, 3 * R), BF16),
            vmem((2 * R, 4 * R), BF16),
            vmem((R, R), BF16),
            vmem((4, R, 128), F32),
            vmem((2, 8, R), F32),
            vmem((8, R), F32),
            vmem((4, 8, R), F32),
            vmem((8, R), F32),
            vmem((2, 8, R), F32),
            vmem((2, 8, R), F32),
            vmem((2, 8, R), F32),
            vmem((6, 4, 8, R), F32),
            vmem((R, D), BF16),
            vmem((R, D), BF16),
            vmem((R, D), BF16),
            vmem((R, H), F32),
            vmem((R, H), F32),
            vmem((3, R, D), BF16),
            vmem((2, R, H), BF16),
            vmem((2, R, D), BF16),
            vmem((2, R, D), BF16),
            dma((3,)),
            dma((4, NC)),
            dma((5, 2, NC)),
            dma((2, NC)),
            dma((2, NC)),
            dma((2,)),
            dma((2,)),
            dma((5,)),
            dma((5,)),
            dma((6,)),
            dma((6,)),
            dma((2, NC)),
            dma((2, NC)),
            dma((2, 2, NC)),
            dma((3, 2, NC)),
            dma((2, NC)),
            dma((2,)),
            dma((2,)),
            vmem((2, 8, 128), F32),
            vmem((2, RING, 8, 128), F32),
            dma((2, RING)),
            dma((2, RING)),
            vmem((R,), jnp.int32),
        ],
        compiler_params=pltpu.CompilerParams(
            collective_id=0, has_side_effects=True, vmem_limit_bytes=42 * 1024 * 1024
        ),
    )(logit_scale, *(pltpu.with_memory_space_constraint(a, pltpu.HBM) for a in (image_emb, text_emb, positive)))


def solution(mesh):
    placed = (P(("group", "blk"), None), P(("group", "blk"), None), P(("group", "blk")), P())
    return jax.shard_map(
        on_device,
        mesh=mesh,
        in_specs=placed,
        out_specs=(P(), P(("group", "blk"), None), P(("group", "blk"), None)),
        check_vma=False,
    )
```
